32 devices in a mesh: row: 8 (over z, core), col: 4 (over y, x).
Axes of the slice: x: 2, y: 2, z: 4, core: 2. Of those that a mesh axis runs over, the one named last changes fastest.
Arguments:
- blocks: bfloat16 [32, 48, 128, 128], P('row', 'col'), may hold values from -0.078125 to 0.078125
- columns: int32 [32, 48], P('row', 'col'), may hold values from 0 to 7
- counts: int32 [32, 4], P('row', 'col'), may hold values from 6 to 12, as said below
- inverse_diag: float32 [32, 128, 128], P('row')
- log_inverse_permeability: float32 [32, 128], P('row'), may hold values from -1 to 1
- base_velocity: float32 [32, 128], P('row'), may hold values from -6 to 6
- direction: float32 [32, 32, 128], P(None, 'row'), may hold values from -6 to 6
- obs_rows: int32 [1024], P('row'), may hold values from 0 to 3
- obs_weight: float32 [1024, 128], P('row'), may hold values from -0.5 to 0.5
- noise_prec: float32 [1024], P('row'), may hold values from 0.5 to 2
Outputs:
- hessian: float32 [32, 32, 128], P(None, 'row')
- predicted: float32 [32, 1024], P(None, 'row')
The draws below stay inside these ranges and needn't reach their ends.
Inputs may be any that keep to these rules, and one draw needn't show every extreme that they name: `counts`: every index of row has a block row with all 12 slots live in each column group.
All inputs are finite; a program needn't handle non-finite values.
Results may differ from the reference program's by a relative error of at most 0.025.
Values may be sent and summed in bfloat16 or wider, within the bound.
A program may use at most 64 MiB of HBM per device.

```python
import math
import jax
import jax.numpy as jnp
from jax import lax

TRACE_UNKNOWNS = 128
SLOTS = 12
ROWS_PER_INDEX = 4
PARAM_DIRECTIONS = 32
OBS_DEV = 128
NBLK = 32
COLBLK = 8
NOBS = 1024
N_ROW = 8
N_COL = 4


def draw_counts(key, part):
    base = jax.random.randint(key, (NBLK, N_COL), (SLOTS + 1) // 2, SLOTS + 1)
    rows = lax.broadcasted_iota(jnp.int32, (NBLK, N_COL), 0)
    return jnp.where(rows % ROWS_PER_INDEX == 0, SLOTS, base).astype(jnp.int32)


def draw_inverse_diag(key, part):
    key_diag = jax.random.fold_in(key, 11)
    key_off = jax.random.fold_in(key, 12)
    diagonal = jax.random.uniform(key_diag, (NBLK, TRACE_UNKNOWNS), jnp.float32, 0.6, 1.4)
    offdiag = 0.45 * jax.random.normal(key_off, (NBLK, TRACE_UNKNOWNS, TRACE_UNKNOWNS), jnp.float32) / jnp.sqrt(1.0 * TRACE_UNKNOWNS)
    identity = jnp.eye(TRACE_UNKNOWNS, dtype=jnp.float32)
    return (offdiag * (1.0 - identity)[None] + diagonal[:, :, None] * identity[None]).astype(jnp.float32)


def set_ends(entries, stream_key, least, high):
    dims = entries.shape
    index_at = [jax.random.randint(jax.random.fold_in(stream_key, axis), (), 0, dims[axis]) for axis in range(len(dims))]
    entries = entries.at[tuple(index_at)].set(least)
    longest = dims.index(max(dims))
    index_at[longest] = (index_at[longest] + 1) % dims[longest]
    return entries.at[tuple(index_at)].set(high)


def levels(key, extent, shards, low, high):
    def one(axis_at, parts):
        draws = jax.random.uniform(jax.random.fold_in(jax.random.fold_in(key, 6), axis_at), (parts,), jnp.float32, low / len(shards), high / len(shards))
        return jnp.repeat(jnp.exp(draws), extent[axis_at] // parts).reshape((-1,) + (1,) * (len(extent) - axis_at - 1))

    factor_of = one(*shards[0])
    for cut in shards[1:]:
        factor_of = factor_of * one(*cut)
    return factor_of


def noise(key, extent, scale, limit, cuts=(), kind=jnp.bfloat16):
    entries = scale * jax.random.normal(key, extent, jnp.float32)
    if cuts:
        entries = entries * levels(key, extent, cuts, -0.22, 0.18)
    return jnp.clip(entries, -limit, limit).astype(kind)


def setup_inputs(seed: int = 0) -> dict:
    streams_of = jax.random.split(jax.random.key(seed), 11)
    blocks = noise(streams_of[0], (NBLK, N_COL * SLOTS, TRACE_UNKNOWNS, TRACE_UNKNOWNS), (4 * SLOTS * TRACE_UNKNOWNS) ** -0.5, 0.078125, ((0, 8), (1, 4)))
    columns = set_ends(jax.random.randint(streams_of[1], (NBLK, N_COL * SLOTS), 0, COLBLK), jax.random.fold_in(streams_of[1], 1), 0, COLBLK - 1).astype(jnp.int32)
    counts = draw_counts(jax.random.fold_in(streams_of[10], 71), 0)
    inverse_diag = draw_inverse_diag(jax.random.fold_in(streams_of[10], 71), 0)
    log_inverse_permeability = jnp.clip(jax.random.uniform(streams_of[4], (NBLK, TRACE_UNKNOWNS), jnp.float32, -1.0, 1.0) * levels(streams_of[4], (NBLK, TRACE_UNKNOWNS), ((0, 8),), -0.4, 0.0), -1.0, 1.0)
    base_velocity = noise(streams_of[5], (NBLK, TRACE_UNKNOWNS), 1.0, 6.0, ((0, 8),), jnp.float32)
    direction = noise(streams_of[6], (PARAM_DIRECTIONS, NBLK, TRACE_UNKNOWNS), 1.0, 6.0, ((1, 8),), jnp.float32)
    obs_rows = set_ends(jax.random.randint(streams_of[7], (NOBS,), 0, ROWS_PER_INDEX), jax.random.fold_in(streams_of[7], 1), 0, ROWS_PER_INDEX - 1).astype(jnp.int32)
    obs_weight = noise(streams_of[8], (NOBS, TRACE_UNKNOWNS), TRACE_UNKNOWNS ** -0.5, 0.5, ((0, 8),), jnp.float32)
    noise_prec = jnp.clip(jnp.exp(math.log(2.0) - 1.3862944 * jax.random.uniform(streams_of[9], (NOBS,), jnp.float32) ** levels(streams_of[9], (NOBS,), ((0, 8),), -0.2, 0.2)), 0.5, 2.0)
    return {"blocks": blocks, "columns": columns, "counts": counts, "inverse_diag": inverse_diag, "log_inverse_permeability": log_inverse_permeability, "base_velocity": base_velocity, "direction": direction, "obs_rows": obs_rows, "obs_weight": obs_weight, "noise_prec": noise_prec}


def diag_apply(inverse_diag, values):
    return jnp.einsum('iab,sib->sia', inverse_diag, values, precision=lax.Precision.HIGHEST)


def diag_apply_t(inverse_diag, values):
    return jnp.einsum('iba,sib->sia', inverse_diag, values, precision=lax.Precision.HIGHEST)


def reference(blocks, columns, counts, inverse_diag, log_inverse_permeability, base_velocity, direction, obs_rows, obs_weight, noise_prec):
    width = N_COL * SLOTS
    alpha_u = jnp.exp(log_inverse_permeability) * base_velocity
    forcing = -alpha_u[None] * direction
    group_of = (jnp.arange(width) // SLOTS).astype(jnp.int32)
    global_cols = (columns + group_of[None, :] * COLBLK).astype(jnp.int32)
    live = (jnp.arange(width) % SLOTS)[None, :] < jnp.repeat(counts, SLOTS, axis=1)
    block_groups = blocks.reshape(N_ROW, ROWS_PER_INDEX, width, TRACE_UNKNOWNS, TRACE_UNKNOWNS)
    col_groups = global_cols.reshape(N_ROW, ROWS_PER_INDEX, width)
    live_groups = live.reshape(N_ROW, ROWS_PER_INDEX, width)

    def apply_forward(values):
        def single_group(items):
            block_part, col_part, live_part = items
            picked = values[:, col_part].astype(jnp.float32)
            picked = jnp.where(live_part[None, :, :, None], picked, 0.0)
            return jnp.einsum('ikab,sikb->sia', block_part.astype(jnp.float32), picked)
        result = lax.map(single_group, (block_groups, col_groups, live_groups))
        return result.transpose(1, 0, 2, 3).reshape(PARAM_DIRECTIONS, NBLK, TRACE_UNKNOWNS)

    def apply_adjoint(values):
        value_groups = values.reshape(PARAM_DIRECTIONS, N_ROW, ROWS_PER_INDEX, TRACE_UNKNOWNS).transpose(1, 0, 2, 3)

        def single_group(carry, items):
            block_part, col_part, live_part, value_part = items
            terms = jnp.einsum('ikab,sia->sikb', block_part.astype(jnp.float32), value_part.astype(jnp.float32))
            terms = jnp.where(live_part[None, :, :, None], terms, 0.0)
            return carry.at[:, col_part].add(terms), None
        start = jnp.zeros((PARAM_DIRECTIONS, NBLK, TRACE_UNKNOWNS), jnp.float32)
        total, unused = lax.scan(single_group, start, (block_groups, col_groups, live_groups, value_groups))
        return total

    trace_state = diag_apply(inverse_diag, forcing)
    for sweep in range(2):
        trace_state = diag_apply(inverse_diag, forcing - apply_forward(trace_state.astype(jnp.bfloat16)))
    onehot = (obs_rows.reshape(N_ROW, OBS_DEV)[:, :, None] == jnp.arange(ROWS_PER_INDEX)[None, None, :]).astype(jnp.float32)
    weight_values = obs_weight.reshape(N_ROW, OBS_DEV, TRACE_UNKNOWNS)
    sampled_draws = jnp.einsum('zjw,fzvw->fzjv', weight_values, trace_state.reshape(PARAM_DIRECTIONS, N_ROW, ROWS_PER_INDEX, TRACE_UNKNOWNS), precision=lax.Precision.HIGHEST)
    predicted = jnp.sum(sampled_draws * onehot[None], axis=3)
    scaled = predicted * noise_prec.reshape(N_ROW, OBS_DEV)[None]
    coupling = onehot[:, :, :, None] * weight_values[:, :, None, :]
    adjoint_force = -jnp.einsum('scp,cpia->scia', scaled, coupling, precision=lax.Precision.HIGHEST).reshape(PARAM_DIRECTIONS, NBLK, TRACE_UNKNOWNS)
    adjoint = diag_apply_t(inverse_diag, adjoint_force)
    for sweep in range(2):
        adjoint = diag_apply_t(inverse_diag, adjoint_force - apply_adjoint(adjoint.astype(jnp.bfloat16)))
    hessian = -alpha_u[None] * adjoint
    return hessian, predicted.reshape(PARAM_DIRECTIONS, NOBS)
```

```python
import functools

import jax
import jax.numpy as jnp
from jax import lax
from jax.experimental import pallas as pl
from jax.experimental.pallas import tpu as pltpu
from jax.sharding import PartitionSpec as P

F32 = jnp.float32
BF16 = jnp.bfloat16
SWEEPS = 2


def flip(index, bits, size):
    total, bit = 0, 1
    while bit < size:
        digit = lax.rem(lax.div(index, jnp.int32(bit)), jnp.int32(2))
        total = total + bit * (1 - digit if (bits // bit) % 2 else digit)
        bit *= 2
    return total


def split(values):
    high = values.astype(BF16)
    return high, (values - high.astype(F32)).astype(BF16)


def matmul(left, right):
    return lax.dot_general(left, right, (((1,), (0,)), ((), ())), preferred_element_type=F32)


def matmul_t(left, right):
    return lax.dot_general(left, right, (((1,), (1,)), ((), ())), preferred_element_type=F32)


def wide_matmul(values, pair):
    rows, width = values.shape[0], pair.shape[1] // 2
    high = values.astype(BF16).astype(F32)
    both = jnp.concatenate([high, values - high], axis=0).astype(BF16)
    out = matmul(both, pair)
    return out[:rows, :width] + out[:rows, width:] + out[rows:, :width]


def kernel(
    ncol,
    nmem,
    columns_ref,
    counts_ref,
    blocks_hbm,
    diag_ref,
    logperm_ref,
    velocity_ref,
    direction_ref,
    obs_rows_ref,
    obs_weight_ref,
    prec_ref,
    hess_ref,
    pred_ref,
    blk,
    merged,
    diag_f,
    diag_a,
    obs_f,
    obs_a,
    part,
    zf,
    xf,
    rs_out,
    rs_in,
    yb,
    ad_out,
    ad_in,
    za_out,
    za,
    hb,
    pb,
    blk_sem,
    zf_s,
    zf_r,
    xf_s,
    xf_r,
    rs_s,
    rs_r,
    yb_s,
    yb_r,
    ad_s,
    ad_r,
    za_s,
    za_r,
    hb_s,
    hb_r,
    pb_s,
    pb_r,
):
    row = lax.axis_index("row")
    col = lax.axis_index("col")
    quad = lax.div(row, jnp.int32(nmem))
    mem = lax.rem(row, jnp.int32(nmem))
    nrows, nslots, width = blk.shape[0], blk.shape[1], blk.shape[2]
    share = direction_ref.shape[0] // ncol
    nblk = nmem * nrows

    def device(q, k, c):
        return (q * nmem + k, c)

    def copy(src, dst, send, recv, target):
        return pltpu.make_async_remote_copy(
            src_ref=src,
            dst_ref=dst,
            send_sem=send,
            recv_sem=recv,
            device_id=target,
            device_id_type=pl.DeviceIdType.MESH,
        )

    def landed(slot, recv):
        copy(slot, slot, recv, recv, (row, col)).wait_recv()

    def block_row(piece, i):
        return piece[i * share : (i + 1) * share]

    def stack(pieces):
        return jnp.concatenate(pieces, axis=0)

    def diag_apply(pairs, piece):
        return stack([wide_matmul(block_row(piece, i), pairs[i]) for i in range(nrows)])

    barrier = pltpu.get_barrier_semaphore()
    peers = [(flip(quad, f, ncol), mem, col) for f in range(1, ncol)]
    peers += [
        (quad, flip(mem, x, nmem), flip(col, e, ncol))
        for e in range(ncol)
        for x in range(nmem)
        if e or x
    ]
    for q, k, c in peers:
        pl.semaphore_signal(
            barrier, inc=1, device_id=device(q, k, c), device_id_type=pl.DeviceIdType.MESH
        )
    fetches = [
        pltpu.make_async_copy(blocks_hbm.at[i], blk.at[i], blk_sem.at[i]) for i in range(nrows)
    ]
    for fetch in fetches:
        fetch.start()

    alpha = jnp.exp(logperm_ref[...]) * velocity_ref[...]
    for i in range(nrows):
        high, low = split(diag_ref[i].T)
        diag_f[i, :, :width] = high
        diag_f[i, :, width:] = low
    mine = direction_ref[pl.ds(col * share, share)]
    forcing = stack([-alpha[i : i + 1] * mine[:, i, :] for i in range(nrows)])
    base = diag_apply(diag_f, forcing)

    def merge(i):
        fetches[i].wait()
        count = counts_ref[i, 0]
        target = [
            jnp.where(jnp.int32(k) < count, columns_ref[i, k], jnp.int32(-1))
            for k in range(nslots)
        ]

        def body(pair, carry):
            for half in range(2):
                j = pair * 2 + half
                total = jnp.zeros((width, width), F32)
                for k in range(nslots):
                    keep = jnp.where(target[k] == j, jnp.float32(1), jnp.float32(0))
                    total = total + keep * blk[i, k].astype(F32)
                at = pl.ds(pl.multiple_of(j * width, width), width)
                merged[i * width : (i + 1) * width, at] = total.astype(BF16)
            return carry

        lax.fori_loop(0, nblk // 2, body, 0)

    sent = []

    def start(item, when=None):
        if when is None:
            item.start()
        else:
            pl.when(when)(item.start)
        sent.append((item, when))

    def spread_along_row(t, piece):
        zf[t, quad] = piece.astype(BF16)
        for f in range(1, ncol):
            q = flip(quad, f, ncol)
            start(
                copy(
                    zf.at[t, quad],
                    zf.at[t, quad],
                    zf_s.at[t, f],
                    zf_r.at[t, quad],
                    device(q, mem, col),
                )
            )

    def forward_to_column(t):
        for f in range(ncol):
            q = flip(quad, f, ncol)
            if f:
                landed(zf.at[t, q], zf_r.at[t, q])
            for x in range(nmem):
                start(
                    copy(
                        zf.at[t, q],
                        xf.at[t, mem, col],
                        xf_s.at[t, f, x],
                        xf_r.at[t, mem, col],
                        device(quad, flip(mem, x, nmem), q),
                    ),
                    None if x else q != col,
                )
        xf[t, mem, col] = zf[t, col]

    def column_state(t):
        for e in range(ncol):
            for x in range(nmem):
                if e or x:
                    k, c = flip(mem, x, nmem), flip(col, e, ncol)
                    landed(xf.at[t, k, c], xf_r.at[t, k, c])
        lanes = []
        for k in range(nmem):
            pieces = [xf[t, k, c].astype(F32) for c in range(ncol)]
            for i in range(nrows):
                lanes.append(stack([block_row(piece, i) for piece in pieces]))
        return jnp.concatenate(lanes, axis=1).astype(BF16)

    def sum_over_columns(t, terms):
        for c in range(ncol):
            rows = terms[c * share : (c + 1) * share]
            piece = stack([rows[:, i * width : (i + 1) * width] for i in range(nrows)])
            part[t, c] = piece
            rs_out[t, c] = piece.astype(BF16)
        for e in range(1, ncol):
            c = flip(col, e, ncol)
            start(
                copy(
                    rs_out.at[t, c],
                    rs_in.at[t, col],
                    rs_s.at[t, e],
                    rs_r.at[t, col],
                    device(quad, mem, c),
                )
            )
        total = part[t, col]
        for e in range(1, ncol):
            c = flip(col, e, ncol)
            landed(rs_in.at[t, c], rs_r.at[t, c])
            total = total + rs_in[t, c].astype(F32)
        return total

    def gather_start(buf, at, send, recv):
        for e in range(1, ncol):
            start(
                copy(
                    buf.at[at + (col,)],
                    buf.at[at + (col,)],
                    send.at[at + (e,)],
                    recv.at[at + (col,)],
                    device(quad, mem, flip(col, e, ncol)),
                )
            )

    def gather_wait(buf, at, recv):
        for e in range(1, ncol):
            c = flip(col, e, ncol)
            landed(buf.at[at + (c,)], recv.at[at + (c,)])

    state = base
    for t in range(SWEEPS):
        if t == 0:
            pl.semaphore_wait(barrier, len(peers))
        spread_along_row(t, state)
        if t == 0:
            for i in range(nrows // 2):
                merge(i)
        forward_to_column(t)
        if t == 0:
            for i in range(nrows // 2, nrows):
                merge(i)
        terms = matmul_t(column_state(t), merged[...])
        if t == 0:
            for i in range(nrows):
                high, low = split(diag_ref[i])
                diag_a[i, :, :width] = high
                diag_a[i, :, width:] = low
            high, low = split(obs_weight_ref[...])
            points = obs_weight_ref.shape[0]
            obs_a[:, :width] = high
            obs_a[:, width:] = low
            high, low = split(obs_weight_ref[...].T)
            obs_f[:, :points] = high
            obs_f[:, points:] = low
        state = base - diag_apply(diag_f, sum_over_columns(t, terms))

    sampled = wide_matmul(state, obs_f[...])
    chosen = [(obs_rows_ref[...] == i).astype(F32) for i in range(nrows)]
    predicted = sum(block_row(sampled, i) * chosen[i] for i in range(nrows))
    weighted = predicted * prec_ref[...]
    force = -wide_matmul(stack([weighted * chosen[i] for i in range(nrows)]), obs_a[...])
    adjoint = diag_apply(diag_a, force)

    for t in range(SWEEPS):
        yb[t, col] = adjoint.astype(BF16)
        gather_start(yb, (t,), yb_s, yb_r)
        if t == 0:
            pb[col] = predicted
            gather_start(pb, (), pb_s, pb_r)
        gather_wait(yb, (t,), yb_r)
        pieces = [yb[t, c].astype(F32) for c in range(ncol)]
        lanes = [stack([block_row(piece, i) for piece in pieces]) for i in range(nrows)]
        terms = matmul(jnp.concatenate(lanes, axis=1).astype(BF16), merged[...])
        for k in range(nmem):
            for c in range(ncol):
                rows = terms[c * share : (c + 1) * share]
                ad_out[t, k, c] = stack(
                    [
                        rows[:, (k * nrows + i) * width : (k * nrows + i + 1) * width]
                        for i in range(nrows)
                    ]
                ).astype(BF16)
        for e in range(ncol):
            for x in range(nmem):
                if e or x:
                    k, c = flip(mem, x, nmem), flip(col, e, ncol)
                    start(
                        copy(
                            ad_out.at[t, k, c],
                            ad_in.at[t, mem, col],
                            ad_s.at[t, x, e],
                            ad_r.at[t, mem, col],
                            device(quad, k, c),
                        )
                    )
        ad_in[t, mem, col] = ad_out[t, mem, col]
        for e in range(ncol):
            c = flip(col, e, ncol)
            for x in range(nmem):
                if e or x:
                    k = flip(mem, x, nmem)
                    landed(ad_in.at[t, k, c], ad_r.at[t, k, c])
            total = sum(ad_in[t, k, c].astype(F32) for k in range(nmem))
            za_out[t, c] = total.astype(BF16)
            start(
                copy(
                    za_out.at[t, c],
                    za.at[t, quad],
                    za_s.at[t, e],
                    za_r.at[t, quad],
                    device(c, mem, col),
                ),
                c != quad,
            )
        total = za_out[t, quad].astype(F32)
        for f in range(1, ncol):
            q = flip(quad, f, ncol)
            landed(za.at[t, q], za_r.at[t, q])
            total = total + za[t, q].astype(F32)
        adjoint = diag_apply(diag_a, force - total)

    hb[col] = stack(
        [-alpha[i : i + 1] * block_row(adjoint, i) for i in range(nrows)]
    ).astype(BF16)
    gather_start(hb, (), hb_s, hb_r)
    gather_wait(pb, (), pb_r)
    for c in range(ncol):
        pred_ref[c * share : (c + 1) * share, :] = pb[c]
    gather_wait(hb, (), hb_r)
    for c in range(ncol):
        piece = hb[c].astype(F32)
        for i in range(nrows):
            hess_ref[c * share : (c + 1) * share, i, :] = block_row(piece, i)

    for item, when in sent:
        if when is None:
            item.wait_send()
        else:
            pl.when(when)(item.wait_send)


def per_device(
    blocks,
    columns,
    counts,
    inverse_diag,
    log_inverse_permeability,
    base_velocity,
    direction,
    obs_rows,
    obs_weight,
    noise_prec,
):
    ncol = lax.axis_size("col")
    nmem = lax.axis_size("row") // ncol
    nrows, nslots, width, _ = blocks.shape
    directions, points = direction.shape[0], obs_weight.shape[0]
    share = directions // ncol
    rows = nrows * share
    dma = pltpu.SemaphoreType.DMA
    vmem = pl.BlockSpec(memory_space=pltpu.VMEM)
    smem = pl.BlockSpec(memory_space=pltpu.SMEM)

    def pieces(*lead):
        return pltpu.VMEM(lead + (rows, width), BF16)

    s, c, g = SWEEPS, ncol, nmem
    return pl.pallas_call(
        functools.partial(kernel, ncol, nmem),
        out_shape=(
            jax.ShapeDtypeStruct(direction.shape, F32),
            jax.ShapeDtypeStruct((directions, points), F32),
        ),
        in_specs=[smem, smem, pl.BlockSpec(memory_space=pl.ANY)] + [vmem] * 7,
        out_specs=(vmem, vmem),
        scratch_shapes=[
            pltpu.VMEM(blocks.shape, BF16),
            pltpu.VMEM((nrows * width, nmem * nrows * width), BF16),
            pltpu.VMEM((nrows, width, 2 * width), BF16),
            pltpu.VMEM((nrows, width, 2 * width), BF16),
            pltpu.VMEM((width, 2 * points), BF16),
            pltpu.VMEM((points, 2 * width), BF16),
            pltpu.VMEM((s, c, rows, width), F32),
            pieces(s, c),
            pieces(s, g, c),
            pieces(s, c),
            pieces(s, c),
            pieces(s, c),
            pieces(s, g, c),
            pieces(s, g, c),
            pieces(s, c),
            pieces(s, c),
            pieces(c),
            pltpu.VMEM((c, share, points), F32),
            dma((nrows,)),
            dma((s, c)),
            dma((s, c)),
            dma((s, c, g)),
            dma((s, g, c)),
            dma((s, c)),
            dma((s, c)),
            dma((s, c)),
            dma((s, c)),
            dma((s, g, c)),
            dma((s, g, c)),
            dma((s, c)),
            dma((s, c)),
            dma((c,)),
            dma((c,)),
            dma((c,)),
            dma((c,)),
        ],
        compiler_params=pltpu.CompilerParams(
            collective_id=0, has_side_effects=True, vmem_limit_bytes=32 * 1024 * 1024
        ),
    )(
        columns,
        counts,
        blocks,
        inverse_diag,
        log_inverse_permeability,
        base_velocity,
        direction,
        obs_rows.reshape(1, points),
        obs_weight,
        noise_prec.reshape(1, points),
    )


def solution(mesh):
    placed = (
        P("row", "col", None, None),
        P("row", "col"),
        P("row", "col"),
        P("row", None, None),
        P("row", None),
        P("row", None),
        P(None, "row", None),
        P("row"),
        P("row", None),
        P("row"),
    )
    return jax.shard_map(
        per_device,
        mesh=mesh,
        in_specs=placed,
        out_specs=(P(None, "row", None), P(None, "row")),
        check_vma=False,
    )
```

```python
import functools

import jax
import jax.numpy as jnp
from jax import lax
from jax.experimental import pallas as pl
from jax.experimental.pallas import tpu as pltpu
from jax.sharding import PartitionSpec as P

F32 = jnp.float32
BF16 = jnp.bfloat16
SWEEPS = 2


def flip(index, bits, size):
    total, bit = 0, 1
    while bit < size:
        digit = lax.rem(lax.div(index, jnp.int32(bit)), jnp.int32(2))
        total = total + bit * (1 - digit if (bits // bit) % 2 else digit)
        bit *= 2
    return total


def split(values):
    high = values.astype(BF16)
    return high, (values - high.astype(F32)).astype(BF16)


def matmul(left, right):
    return lax.dot_general(left, right, (((1,), (0,)), ((), ())), preferred_element_type=F32)


def matmul_t(left, right):
    return lax.dot_general(left, right, (((1,), (1,)), ((), ())), preferred_element_type=F32)


def wide_matmul(values, pair):
    rows, width = values.shape[0], pair.shape[1] // 2
    high = values.astype(BF16).astype(F32)
    both = jnp.concatenate([high, values - high], axis=0).astype(BF16)
    out = matmul(both, pair)
    return out[:rows, :width] + out[:rows, width:] + out[rows:, :width]


def kernel(
    ncol,
    nmem,
    columns_hbm,
    counts_hbm,
    blocks_hbm,
    diag_hbm,
    logperm_hbm,
    velocity_hbm,
    direction_hbm,
    obs_rows_hbm,
    obs_weight_hbm,
    prec_hbm,
    hess_ref,
    pred_ref,
    columns_ref,
    counts_ref,
    diag_ref,
    logperm_ref,
    velocity_ref,
    direction_ref,
    obs_rows_ref,
    obs_weight_ref,
    prec_ref,
    blk,
    merged,
    diag_f,
    diag_a,
    obs_f,
    obs_a,
    part,
    zf,
    xf,
    rs_out,
    rs_in,
    yb,
    ad_out,
    ad_in,
    za_out,
    za,
    hb,
    pb,
    in_sem,
    blk_sem,
    zf_s,
    zf_r,
    xf_s,
    xf_r,
    rs_s,
    rs_r,
    yb_s,
    yb_r,
    ad_s,
    ad_r,
    za_s,
    za_r,
    hb_s,
    hb_r,
    pb_s,
    pb_r,
):
    row = lax.axis_index("row")
    col = lax.axis_index("col")
    quad = lax.div(row, jnp.int32(nmem))
    mem = lax.rem(row, jnp.int32(nmem))
    nrows, nslots, width = blk.shape[0], blk.shape[1], blk.shape[2]
    share = direction_ref.shape[0]
    nblk = nmem * nrows

    def device(q, k, c):
        return (q * nmem + k, c)

    def copy(src, dst, send, recv, target):
        return pltpu.make_async_remote_copy(
            src_ref=src,
            dst_ref=dst,
            send_sem=send,
            recv_sem=recv,
            device_id=target,
            device_id_type=pl.DeviceIdType.MESH,
        )

    def landed(slot, recv):
        copy(slot, slot, recv, recv, (row, col)).wait_recv()

    def block_row(piece, i):
        return piece[i * share : (i + 1) * share]

    def stack(pieces):
        return jnp.concatenate(pieces, axis=0)

    def diag_apply(pairs, piece):
        return stack([wide_matmul(block_row(piece, i), pairs[i]) for i in range(nrows)])

    barrier = pltpu.get_barrier_semaphore()
    peers = [(flip(quad, f, ncol), mem, col) for f in range(1, ncol)]
    peers += [
        (quad, flip(mem, x, nmem), flip(col, e, ncol))
        for e in range(ncol)
        for x in range(nmem)
        if e or x
    ]
    for q, k, c in peers:
        pl.semaphore_signal(
            barrier, inc=1, device_id=device(q, k, c), device_id_type=pl.DeviceIdType.MESH
        )
    sources = (
        (logperm_hbm, logperm_ref),
        (velocity_hbm, velocity_ref),
        (direction_hbm.at[pl.ds(col * share, share)], direction_ref),
        (diag_hbm, diag_ref),
        (columns_hbm, columns_ref),
        (counts_hbm, counts_ref),
        (obs_rows_hbm, obs_rows_ref),
        (obs_weight_hbm, obs_weight_ref),
        (prec_hbm, prec_ref),
    )
    inputs = [
        pltpu.make_async_copy(src, dst, in_sem.at[n]) for n, (src, dst) in enumerate(sources)
    ]
    for item in inputs:
        item.start()
    fetches = [
        pltpu.make_async_copy(blocks_hbm.at[i], blk.at[i], blk_sem.at[i]) for i in range(nrows)
    ]
    for fetch in fetches:
        fetch.start()

    for item in inputs[:4]:
        item.wait()
    alpha = jnp.exp(logperm_ref[...]) * velocity_ref[...]
    for i in range(nrows):
        high, low = split(diag_ref[i].T)
        diag_f[i, :, :width] = high
        diag_f[i, :, width:] = low
    mine = direction_ref[...]
    forcing = stack([-alpha[i : i + 1] * mine[:, i, :] for i in range(nrows)])
    base = diag_apply(diag_f, forcing)

    def merge(i):
        fetches[i].wait()
        count = counts_ref[0, i]
        target = [
            jnp.where(jnp.int32(k) < count, columns_ref[i, k], jnp.int32(-1))
            for k in range(nslots)
        ]

        def body(pair, carry):
            for half in range(2):
                j = pair * 2 + half
                total = jnp.zeros((width, width), F32)
                for k in range(nslots):
                    keep = jnp.where(target[k] == j, jnp.float32(1), jnp.float32(0))
                    total = total + keep * blk[i, k].astype(F32)
                at = pl.ds(pl.multiple_of(j * width, width), width)
                merged[i * width : (i + 1) * width, at] = total.astype(BF16)
            return carry

        lax.fori_loop(0, nblk // 2, body, 0)

    sent = []

    def start(item, when=None):
        if when is None:
            item.start()
        else:
            pl.when(when)(item.start)
        sent.append((item, when))

    def drain(items):
        for item, when in items:
            if when is None:
                item.wait_send()
            else:
                pl.when(when)(item.wait_send)

    def spread_along_row(t, piece):
        zf[t, quad] = piece.astype(BF16)
        for f in range(1, ncol):
            q = flip(quad, f, ncol)
            start(
                copy(
                    zf.at[t, quad],
                    zf.at[t, quad],
                    zf_s.at[t, f],
                    zf_r.at[t, quad],
                    device(q, mem, col),
                )
            )

    def forward_to_column(t):
        for f in range(ncol):
            q = flip(quad, f, ncol)
            if f:
                landed(zf.at[t, q], zf_r.at[t, q])
            for x in range(nmem):
                start(
                    copy(
                        zf.at[t, q],
                        xf.at[t, mem, col],
                        xf_s.at[t, f, x],
                        xf_r.at[t, mem, col],
                        device(quad, flip(mem, x, nmem), q),
                    ),
                    None if x else q != col,
                )
        xf[t, mem, col] = zf[t, col]

    def column_state(t):
        for e in range(ncol):
            for x in range(nmem):
                if e or x:
                    k, c = flip(mem, x, nmem), flip(col, e, ncol)
                    landed(xf.at[t, k, c], xf_r.at[t, k, c])
        lanes = []
        for k in range(nmem):
            pieces = [xf[t, k, c].astype(F32) for c in range(ncol)]
            for i in range(nrows):
                lanes.append(stack([block_row(piece, i) for piece in pieces]))
        return jnp.concatenate(lanes, axis=1).astype(BF16)

    def sum_over_columns(t, terms):
        for c in range(ncol):
            rows = terms[c * share : (c + 1) * share]
            piece = stack([rows[:, i * width : (i + 1) * width] for i in range(nrows)])
            part[t, c] = piece
            rs_out[t, c] = piece.astype(BF16)
        for e in range(1, ncol):
            c = flip(col, e, ncol)
            start(
                copy(
                    rs_out.at[t, c],
                    rs_in.at[t, col],
                    rs_s.at[t, e],
                    rs_r.at[t, col],
                    device(quad, mem, c),
                )
            )
        total = part[t, col]
        for e in range(1, ncol):
            c = flip(col, e, ncol)
            landed(rs_in.at[t, c], rs_r.at[t, c])
            total = total + rs_in[t, c].astype(F32)
        return total

    def gather_start(buf, at, send, recv):
        for e in range(1, ncol):
            start(
                copy(
                    buf.at[at + (col,)],
                    buf.at[at + (col,)],
                    send.at[at + (e,)],
                    recv.at[at + (col,)],
                    device(quad, mem, flip(col, e, ncol)),
                )
            )

    def gather_wait(buf, at, recv):
        for e in range(1, ncol):
            c = flip(col, e, ncol)
            landed(buf.at[at + (c,)], recv.at[at + (c,)])

    state = base
    for t in range(SWEEPS):
        if t == 0:
            pl.semaphore_wait(barrier, len(peers))
        spread_along_row(t, state)
        if t == 0:
            for item in inputs[4:]:
                item.wait()
            for i in range(nrows // 2):
                merge(i)
        forward_to_column(t)
        if t == 0:
            for i in range(nrows // 2, nrows):
                merge(i)
        terms = matmul_t(column_state(t), merged[...])
        if t == 0:
            for i in range(nrows):
                high, low = split(diag_ref[i])
                diag_a[i, :, :width] = high
                diag_a[i, :, width:] = low
            high, low = split(obs_weight_ref[...])
            points = obs_weight_ref.shape[0]
            obs_a[:, :width] = high
            obs_a[:, width:] = low
            high, low = split(obs_weight_ref[...].T)
            obs_f[:, :points] = high
            obs_f[:, points:] = low
        state = base - diag_apply(diag_f, sum_over_columns(t, terms))

    sampled = wide_matmul(state, obs_f[...])
    chosen = [(obs_rows_ref[...] == i).astype(F32) for i in range(nrows)]
    predicted = sum(block_row(sampled, i) * chosen[i] for i in range(nrows))
    weighted = predicted * prec_ref[...]
    force = -wide_matmul(stack([weighted * chosen[i] for i in range(nrows)]), obs_a[...])
    adjoint = diag_apply(diag_a, force)

    for t in range(SWEEPS):
        yb[t, col] = adjoint.astype(BF16)
        gather_start(yb, (t,), yb_s, yb_r)
        if t == 0:
            pb[col] = predicted
            gather_start(pb, (), pb_s, pb_r)
        gather_wait(yb, (t,), yb_r)
        pieces = [yb[t, c].astype(F32) for c in range(ncol)]
        lanes = [stack([block_row(piece, i) for piece in pieces]) for i in range(nrows)]
        terms = matmul(jnp.concatenate(lanes, axis=1).astype(BF16), merged[...])
        for k in range(nmem):
            for c in range(ncol):
                rows = terms[c * share : (c + 1) * share]
                ad_out[t, k, c] = stack(
                    [
                        rows[:, (k * nrows + i) * width : (k * nrows + i + 1) * width]
                        for i in range(nrows)
                    ]
                ).astype(BF16)
        for e in range(ncol):
            for x in range(nmem):
                if e or x:
                    k, c = flip(mem, x, nmem), flip(col, e, ncol)
                    start(
                        copy(
                            ad_out.at[t, k, c],
                            ad_in.at[t, mem, col],
                            ad_s.at[t, x, e],
                            ad_r.at[t, mem, col],
                            device(quad, k, c),
                        )
                    )
        ad_in[t, mem, col] = ad_out[t, mem, col]
        for e in range(ncol):
            c = flip(col, e, ncol)
            for x in range(nmem):
                if e or x:
                    k = flip(mem, x, nmem)
                    landed(ad_in.at[t, k, c], ad_r.at[t, k, c])
            total = sum(ad_in[t, k, c].astype(F32) for k in range(nmem))
            za_out[t, c] = total.astype(BF16)
            start(
                copy(
                    za_out.at[t, c],
                    za.at[t, quad],
                    za_s.at[t, e],
                    za_r.at[t, quad],
                    device(c, mem, col),
                ),
                c != quad,
            )
        total = za_out[t, quad].astype(F32)
        for f in range(1, ncol):
            q = flip(quad, f, ncol)
            landed(za.at[t, q], za_r.at[t, q])
            total = total + za[t, q].astype(F32)
        adjoint = diag_apply(diag_a, force - total)

    hb[col] = stack(
        [-alpha[i : i + 1] * block_row(adjoint, i) for i in range(nrows)]
    ).astype(BF16)
    gather_start(hb, (), hb_s, hb_r)
    gather_wait(pb, (), pb_r)
    for c in range(ncol):
        pred_ref[c * share : (c + 1) * share, :] = pb[c]
    drain(sent[: 1 - ncol])
    gather_wait(hb, (), hb_r)
    for c in range(ncol):
        piece = hb[c].astype(F32)
        for i in range(nrows):
            hess_ref[c * share : (c + 1) * share, i, :] = block_row(piece, i)

    drain(sent[1 - ncol :])


def per_device(
    blocks,
    columns,
    counts,
    inverse_diag,
    log_inverse_permeability,
    base_velocity,
    direction,
    obs_rows,
    obs_weight,
    noise_prec,
):
    ncol = lax.axis_size("col")
    nmem = lax.axis_size("row") // ncol
    nrows, nslots, width, _ = blocks.shape
    directions, points = direction.shape[0], obs_weight.shape[0]
    share = directions // ncol
    rows = nrows * share
    dma = pltpu.SemaphoreType.DMA
    vmem = pl.BlockSpec(memory_space=pltpu.VMEM)

    def pieces(*lead):
        return pltpu.VMEM(lead + (rows, width), BF16)

    s, c, g = SWEEPS, ncol, nmem
    return pl.pallas_call(
        functools.partial(kernel, ncol, nmem),
        out_shape=(
            jax.ShapeDtypeStruct(direction.shape, F32),
            jax.ShapeDtypeStruct((directions, points), F32),
        ),
        in_specs=[pl.BlockSpec(memory_space=pl.ANY)] * 10,
        out_specs=(vmem, vmem),
        scratch_shapes=[
            pltpu.SMEM(columns.shape, jnp.int32),
            pltpu.SMEM((1, nrows), jnp.int32),
            pltpu.VMEM(inverse_diag.shape, F32),
            pltpu.VMEM(base_velocity.shape, F32),
            pltpu.VMEM(base_velocity.shape, F32),
            pltpu.VMEM((share,) + direction.shape[1:], F32),
            pltpu.VMEM((1, points), jnp.int32),
            pltpu.VMEM(obs_weight.shape, F32),
            pltpu.VMEM((1, points), F32),
            pltpu.VMEM(blocks.shape, BF16),
            pltpu.VMEM((nrows * width, nmem * nrows * width), BF16),
            pltpu.VMEM((nrows, width, 2 * width), BF16),
            pltpu.VMEM((nrows, width, 2 * width), BF16),
            pltpu.VMEM((width, 2 * points), BF16),
            pltpu.VMEM((points, 2 * width), BF16),
            pltpu.VMEM((s, c, rows, width), F32),
            pieces(s, c),
            pieces(s, g, c),
            pieces(s, c),
            pieces(s, c),
            pieces(s, c),
            pieces(s, g, c),
            pieces(s, g, c),
            pieces(s, c),
            pieces(s, c),
            pieces(c),
            pltpu.VMEM((c, share, points), F32),
            dma((9,)),
            dma((nrows,)),
            dma((s, c)),
            dma((s, c)),
            dma((s, c, g)),
            dma((s, g, c)),
            dma((s, c)),
            dma((s, c)),
            dma((s, c)),
            dma((s, c)),
            dma((s, g, c)),
            dma((s, g, c)),
            dma((s, c)),
            dma((s, c)),
            dma((c,)),
            dma((c,)),
            dma((c,)),
            dma((c,)),
        ],
        compiler_params=pltpu.CompilerParams(
            collective_id=0, has_side_effects=True, vmem_limit_bytes=60 * 1024 * 1024
        ),
    )(
        columns,
        counts.reshape(1, nrows),
        blocks,
        inverse_diag,
        log_inverse_permeability,
        base_velocity,
        direction,
        obs_rows.reshape(1, points),
        obs_weight,
        noise_prec.reshape(1, points),
    )


def solution(mesh):
    placed = (
        P("row", "col", None, None),
        P("row", "col"),
        P("row", "col"),
        P("row", None, None),
        P("row", None),
        P("row", None),
        P(None, "row", None),
        P("row"),
        P("row", None),
        P("row"),
    )
    return jax.shard_map(
        per_device,
        mesh=mesh,
        in_specs=placed,
        out_specs=(P(None, "row", None), P(None, "row")),
        check_vma=False,
    )
```

```python
import functools

import jax
import jax.numpy as jnp
from jax import lax
from jax.experimental import pallas as pl
from jax.experimental.pallas import tpu as pltpu
from jax.sharding import PartitionSpec as P

F32 = jnp.float32
BF16 = jnp.bfloat16
SWEEPS = 2


def flip(index, bits, size):
    total, bit = 0, 1
    while bit < size:
        digit = lax.rem(lax.div(index, jnp.int32(bit)), jnp.int32(2))
        total = total + bit * (1 - digit if (bits // bit) % 2 else digit)
        bit *= 2
    return total


def split(values):
    high = values.astype(BF16)
    return high, (values - high.astype(F32)).astype(BF16)


def matmul(left, right):
    return lax.dot_general(left, right, (((1,), (0,)), ((), ())), preferred_element_type=F32)


def matmul_t(left, right):
    return lax.dot_general(left, right, (((1,), (1,)), ((), ())), preferred_element_type=F32)


def wide_matmul(values, pair):
    rows, width = values.shape[0], pair.shape[1] // 2
    high = values.astype(BF16).astype(F32)
    both = jnp.concatenate([high, values - high], axis=0).astype(BF16)
    out = matmul(both, pair)
    return out[:rows, :width] + out[:rows, width:] + out[rows:, :width]


def kernel(
    ncol,
    nmem,
    columns_hbm,
    counts_hbm,
    blocks_hbm,
    diag_hbm,
    logperm_hbm,
    velocity_hbm,
    direction_hbm,
    obs_rows_hbm,
    obs_weight_hbm,
    prec_hbm,
    hess_ref,
    pred_ref,
    columns_ref,
    counts_ref,
    diag_ref,
    logperm_ref,
    velocity_ref,
    direction_ref,
    obs_rows_ref,
    obs_weight_ref,
    prec_ref,
    blk,
    merged,
    diag_f,
    diag_a,
    obs_f,
    obs_a,
    part,
    zf,
    xf,
    rs_out,
    rs_in,
    yb,
    ad_out,
    ad_in,
    hb,
    pb,
    in_sem,
    blk_sem,
    zf_s,
    zf_r,
    xf_s,
    xf_r,
    rs_s,
    rs_r,
    yb_s,
    yb_r,
    ad_s,
    ad_r,
    hb_s,
    hb_r,
    pb_s,
    pb_r,
):
    row = lax.axis_index("row")
    col = lax.axis_index("col")
    quad = lax.div(row, jnp.int32(nmem))
    mem = lax.rem(row, jnp.int32(nmem))
    nrows, nslots, width = blk.shape[0], blk.shape[1], blk.shape[2]
    share = direction_ref.shape[0]
    nblk = nmem * nrows

    def device(q, k, c):
        return (q * nmem + k, c)

    def copy(src, dst, send, recv, target):
        return pltpu.make_async_remote_copy(
            src_ref=src,
            dst_ref=dst,
            send_sem=send,
            recv_sem=recv,
            device_id=target,
            device_id_type=pl.DeviceIdType.MESH,
        )

    def landed(slot, recv):
        copy(slot, slot, recv, recv, (row, col)).wait_recv()

    def block_row(piece, i):
        return piece[i * share : (i + 1) * share]

    def stack(pieces):
        return jnp.concatenate(pieces, axis=0)

    def diag_apply(pairs, piece):
        return stack([wide_matmul(block_row(piece, i), pairs[i]) for i in range(nrows)])

    barrier = pltpu.get_barrier_semaphore()
    peers = [((quad, mem, flip(col, e, ncol)), None) for e in range(1, ncol)]
    peers += [((flip(quad, f, ncol), mem, col), None) for f in range(1, ncol)]
    peers += [
        ((quad, flip(mem, x, nmem), flip(col, e, ncol)), None)
        for e in range(ncol)
        for x in range(1, nmem)
    ]
    off = quad != col
    for f in range(ncol):
        for x in range(nmem):
            when = None if f or x else off
            peers.append(((flip(quad, f, ncol), flip(mem, x, nmem), quad), when))
            peers.append(((col, flip(mem, x, nmem), flip(col, f, ncol)), when))

    def greet(target):
        pl.semaphore_signal(
            barrier, inc=1, device_id=device(*target), device_id_type=pl.DeviceIdType.MESH
        )

    for target, when in peers:
        if when is None:
            greet(target)
        else:
            pl.when(when)(functools.partial(greet, target))
    greeted = sum(1 if when is None else when.astype(jnp.int32) for _, when in peers)
    sources = (
        (logperm_hbm, logperm_ref),
        (velocity_hbm, velocity_ref),
        (direction_hbm.at[pl.ds(col * share, share)], direction_ref),
        (diag_hbm, diag_ref),
        (columns_hbm, columns_ref),
        (counts_hbm, counts_ref),
        (obs_rows_hbm, obs_rows_ref),
        (obs_weight_hbm, obs_weight_ref),
        (prec_hbm, prec_ref),
    )
    inputs = [
        pltpu.make_async_copy(src, dst, in_sem.at[n]) for n, (src, dst) in enumerate(sources)
    ]
    for item in inputs:
        item.start()
    fetches = [
        pltpu.make_async_copy(blocks_hbm.at[i], blk.at[i], blk_sem.at[i]) for i in range(nrows)
    ]
    for fetch in fetches:
        fetch.start()

    for item in inputs[:4]:
        item.wait()
    alpha = jnp.exp(logperm_ref[...]) * velocity_ref[...]
    for i in range(nrows):
        high, low = split(diag_ref[i].T)
        diag_f[i, :, :width] = high
        diag_f[i, :, width:] = low
    mine = direction_ref[...]
    forcing = stack([-alpha[i : i + 1] * mine[:, i, :] for i in range(nrows)])
    base = diag_apply(diag_f, forcing)

    def merge(i):
        fetches[i].wait()
        count = counts_ref[0, i]
        target = [
            jnp.where(jnp.int32(k) < count, columns_ref[i, k], jnp.int32(-1))
            for k in range(nslots)
        ]

        def body(pair, carry):
            for half in range(2):
                j = pair * 2 + half
                total = jnp.zeros((width, width), F32)
                for k in range(nslots):
                    keep = jnp.where(target[k] == j, jnp.float32(1), jnp.float32(0))
                    total = total + keep * blk[i, k].astype(F32)
                at = pl.ds(pl.multiple_of(j * width, width), width)
                merged[i * width : (i + 1) * width, at] = total.astype(BF16)
            return carry

        lax.fori_loop(0, nblk // 2, body, 0)

    sent = []

    def start(item, when=None):
        if when is None:
            item.start()
        else:
            pl.when(when)(item.start)
        sent.append((item, when))

    def drain(items):
        for item, when in items:
            if when is None:
                item.wait_send()
            else:
                pl.when(when)(item.wait_send)

    def spread_along_row(t, piece):
        zf[t, quad] = piece.astype(BF16)
        for f in range(1, ncol):
            q = flip(quad, f, ncol)
            start(
                copy(
                    zf.at[t, quad],
                    zf.at[t, quad],
                    zf_s.at[t, f],
                    zf_r.at[t, quad],
                    device(q, mem, col),
                )
            )

    def forward_to_column(t):
        for f in range(ncol):
            q = flip(quad, f, ncol)
            if f:
                landed(zf.at[t, q], zf_r.at[t, q])
            for x in range(nmem):
                start(
                    copy(
                        zf.at[t, q],
                        xf.at[t, mem, col],
                        xf_s.at[t, f, x],
                        xf_r.at[t, mem, col],
                        device(quad, flip(mem, x, nmem), q),
                    ),
                    None if x else q != col,
                )
        xf[t, mem, col] = zf[t, col]

    def column_state(t):
        for e in range(ncol):
            for x in range(nmem):
                if e or x:
                    k, c = flip(mem, x, nmem), flip(col, e, ncol)
                    landed(xf.at[t, k, c], xf_r.at[t, k, c])
        lanes = []
        for k in range(nmem):
            pieces = [xf[t, k, c].astype(F32) for c in range(ncol)]
            for i in range(nrows):
                lanes.append(stack([block_row(piece, i) for piece in pieces]))
        return jnp.concatenate(lanes, axis=1).astype(BF16)

    def sum_over_columns(t, terms):
        for c in range(ncol):
            rows = terms[c * share : (c + 1) * share]
            piece = stack([rows[:, i * width : (i + 1) * width] for i in range(nrows)])
            part[t, c] = piece
            rs_out[t, c] = piece.astype(BF16)
        for e in range(1, ncol):
            c = flip(col, e, ncol)
            start(
                copy(
                    rs_out.at[t, c],
                    rs_in.at[t, col],
                    rs_s.at[t, e],
                    rs_r.at[t, col],
                    device(quad, mem, c),
                )
            )
        total = part[t, col]
        for e in range(1, ncol):
            c = flip(col, e, ncol)
            landed(rs_in.at[t, c], rs_r.at[t, c])
            total = total + rs_in[t, c].astype(F32)
        return total

    def gather_start(buf, at, send, recv):
        for e in range(1, ncol):
            start(
                copy(
                    buf.at[at + (col,)],
                    buf.at[at + (col,)],
                    send.at[at + (e,)],
                    recv.at[at + (col,)],
                    device(quad, mem, flip(col, e, ncol)),
                )
            )

    def gather_wait(buf, at, recv):
        for e in range(1, ncol):
            c = flip(col, e, ncol)
            landed(buf.at[at + (c,)], recv.at[at + (c,)])

    state = base
    for t in range(SWEEPS):
        if t == 0:
            pl.semaphore_wait(barrier, greeted)
        spread_along_row(t, state)
        if t == 0:
            for item in inputs[4:]:
                item.wait()
            for i in range(nrows // 2):
                merge(i)
        forward_to_column(t)
        if t == 0:
            for i in range(nrows // 2, nrows):
                merge(i)
        terms = matmul_t(column_state(t), merged[...])
        if t == 0:
            for i in range(nrows):
                high, low = split(diag_ref[i])
                diag_a[i, :, :width] = high
                diag_a[i, :, width:] = low
            high, low = split(obs_weight_ref[...])
            points = obs_weight_ref.shape[0]
            obs_a[:, :width] = high
            obs_a[:, width:] = low
            high, low = split(obs_weight_ref[...].T)
            obs_f[:, :points] = high
            obs_f[:, points:] = low
        state = base - diag_apply(diag_f, sum_over_columns(t, terms))

    sampled = wide_matmul(state, obs_f[...])
    chosen = [(obs_rows_ref[...] == i).astype(F32) for i in range(nrows)]
    predicted = sum(block_row(sampled, i) * chosen[i] for i in range(nrows))
    weighted = predicted * prec_ref[...]
    force = -wide_matmul(stack([weighted * chosen[i] for i in range(nrows)]), obs_a[...])
    adjoint = diag_apply(diag_a, force)

    for t in range(SWEEPS):
        yb[t, col] = adjoint.astype(BF16)
        gather_start(yb, (t,), yb_s, yb_r)
        if t == 0:
            pb[col] = predicted
            gather_start(pb, (), pb_s, pb_r)
        gather_wait(yb, (t,), yb_r)
        pieces = [yb[t, c].astype(F32) for c in range(ncol)]
        lanes = [stack([block_row(piece, i) for piece in pieces]) for i in range(nrows)]
        terms = matmul(jnp.concatenate(lanes, axis=1).astype(BF16), merged[...])
        for k in range(nmem):
            for c in range(ncol):
                rows = terms[c * share : (c + 1) * share]
                ad_out[t, k, c] = stack(
                    [
                        rows[:, (k * nrows + i) * width : (k * nrows + i + 1) * width]
                        for i in range(nrows)
                    ]
                ).astype(BF16)
        for e in reversed(range(ncol)):
            for x in range(nmem):
                k, c = flip(mem, x, nmem), flip(col, e, ncol)
                start(
                    copy(
                        ad_out.at[t, k, c],
                        ad_in.at[t, mem, quad],
                        ad_s.at[t, x, e],
                        ad_r.at[t, mem, quad],
                        device(col, k, c),
                    ),
                    None if e or x else off,
                )

        @pl.when(quad == col)
        def _():
            ad_in[t, mem, quad] = ad_out[t, mem, col]

        total = 0.0
        for f in range(ncol):
            for x in range(nmem):
                k, q = flip(mem, x, nmem), flip(quad, f, ncol)
                wait = functools.partial(landed, ad_in.at[t, k, q], ad_r.at[t, k, q])
                if f or x:
                    wait()
                else:
                    pl.when(off)(wait)
                total = total + ad_in[t, k, q].astype(F32)
        adjoint = diag_apply(diag_a, force - total)

    hb[col] = stack(
        [-alpha[i : i + 1] * block_row(adjoint, i) for i in range(nrows)]
    ).astype(BF16)
    gather_start(hb, (), hb_s, hb_r)
    gather_wait(pb, (), pb_r)
    for c in range(ncol):
        pred_ref[c * share : (c + 1) * share, :] = pb[c]
    drain(sent[: 1 - ncol])
    gather_wait(hb, (), hb_r)
    for c in range(ncol):
        piece = hb[c].astype(F32)
        for i in range(nrows):
            hess_ref[c * share : (c + 1) * share, i, :] = block_row(piece, i)

    drain(sent[1 - ncol :])


def hand_over(hess_from, pred_from, hess_to, pred_to, sem):
    moves = [
        pltpu.make_async_copy(hess_from, hess_to, sem.at[0]),
        pltpu.make_async_copy(pred_from, pred_to, sem.at[1]),
    ]
    for move in moves:
        move.start()
    for move in moves:
        move.wait()


def per_device(
    blocks,
    columns,
    counts,
    inverse_diag,
    log_inverse_permeability,
    base_velocity,
    direction,
    obs_rows,
    obs_weight,
    noise_prec,
):
    ncol = lax.axis_size("col")
    nmem = lax.axis_size("row") // ncol
    nrows, nslots, width, _ = blocks.shape
    directions, points = direction.shape[0], obs_weight.shape[0]
    share = directions // ncol
    rows = nrows * share
    dma = pltpu.SemaphoreType.DMA
    vmem = pl.BlockSpec(memory_space=pltpu.VMEM)

    def pieces(*lead):
        return pltpu.VMEM(lead + (rows, width), BF16)

    s, c, g = SWEEPS, ncol, nmem
    results = pl.pallas_call(
        functools.partial(kernel, ncol, nmem),
        out_shape=(
            jax.ShapeDtypeStruct(direction.shape, F32),
            jax.ShapeDtypeStruct((directions, points), F32),
        ),
        in_specs=[pl.BlockSpec(memory_space=pl.ANY)] * 10,
        out_specs=(vmem, vmem),
        scratch_shapes=[
            pltpu.SMEM(columns.shape, jnp.int32),
            pltpu.SMEM((1, nrows), jnp.int32),
            pltpu.VMEM(inverse_diag.shape, F32),
            pltpu.VMEM(base_velocity.shape, F32),
            pltpu.VMEM(base_velocity.shape, F32),
            pltpu.VMEM((share,) + direction.shape[1:], F32),
            pltpu.VMEM((1, points), jnp.int32),
            pltpu.VMEM(obs_weight.shape, F32),
            pltpu.VMEM((1, points), F32),
            pltpu.VMEM(blocks.shape, BF16),
            pltpu.VMEM((nrows * width, nmem * nrows * width), BF16),
            pltpu.VMEM((nrows, width, 2 * width), BF16),
            pltpu.VMEM((nrows, width, 2 * width), BF16),
            pltpu.VMEM((width, 2 * points), BF16),
            pltpu.VMEM((points, 2 * width), BF16),
            pltpu.VMEM((s, c, rows, width), F32),
            pieces(s, c),
            pieces(s, g, c),
            pieces(s, c),
            pieces(s, c),
            pieces(s, c),
            pieces(s, g, c),
            pieces(s, g, c),
            pieces(c),
            pltpu.VMEM((c, share, points), F32),
            dma((9,)),
            dma((nrows,)),
            dma((s, c)),
            dma((s, c)),
            dma((s, c, g)),
            dma((s, g, c)),
            dma((s, c)),
            dma((s, c)),
            dma((s, c)),
            dma((s, c)),
            dma((s, g, c)),
            dma((s, g, c)),
            dma((c,)),
            dma((c,)),
            dma((c,)),
            dma((c,)),
        ],
        compiler_params=pltpu.CompilerParams(
            collective_id=0, has_side_effects=True, vmem_limit_bytes=60 * 1024 * 1024
        ),
    )(
        columns,
        counts.reshape(1, nrows),
        blocks,
        inverse_diag,
        log_inverse_permeability,
        base_velocity,
        direction,
        obs_rows.reshape(1, points),
        obs_weight,
        noise_prec.reshape(1, points),
    )
    anywhere = pl.BlockSpec(memory_space=pl.ANY)
    return pl.pallas_call(
        hand_over,
        out_shape=tuple(jax.ShapeDtypeStruct(x.shape, x.dtype) for x in results),
        in_specs=[anywhere] * 2,
        out_specs=(anywhere, anywhere),
        scratch_shapes=[dma((2,))],
        compiler_params=pltpu.CompilerParams(vmem_limit_bytes=60 * 1024 * 1024),
    )(*results)


def solution(mesh):
    placed = (
        P("row", "col", None, None),
        P("row", "col"),
        P("row", "col"),
        P("row", None, None),
        P("row", None),
        P("row", None),
        P(None, "row", None),
        P("row"),
        P("row", None),
        P("row"),
    )
    return jax.shard_map(
        per_device,
        mesh=mesh,
        in_specs=placed,
        out_specs=(P(None, "row", None), P(None, "row")),
        check_vma=False,
    )
```

```python
import functools

import jax
import jax.numpy as jnp
from jax import lax
from jax.experimental import pallas as pl
from jax.experimental.pallas import tpu as pltpu
from jax.sharding import PartitionSpec as P

F32 = jnp.float32
BF16 = jnp.bfloat16
SWEEPS = 2


def flip(index, bits, size):
    total, bit = 0, 1
    while bit < size:
        digit = lax.rem(lax.div(index, jnp.int32(bit)), jnp.int32(2))
        total = total + bit * (1 - digit if (bits // bit) % 2 else digit)
        bit *= 2
    return total


def split(values):
    high = values.astype(BF16)
    return high, (values - high.astype(F32)).astype(BF16)


def matmul(left, right):
    return lax.dot_general(left, right, (((1,), (0,)), ((), ())), preferred_element_type=F32)


def matmul_t(left, right):
    return lax.dot_general(left, right, (((1,), (1,)), ((), ())), preferred_element_type=F32)


def wide_matmul(values, pair):
    rows, width = values.shape[0], pair.shape[1] // 2
    high = values.astype(BF16).astype(F32)
    both = jnp.concatenate([high, values - high], axis=0).astype(BF16)
    out = matmul(both, pair)
    return out[:rows, :width] + out[:rows, width:] + out[rows:, :width]


def kernel(
    ncol,
    nmem,
    columns_hbm,
    counts_hbm,
    blocks_hbm,
    diag_hbm,
    logperm_hbm,
    velocity_hbm,
    direction_hbm,
    obs_rows_hbm,
    obs_weight_hbm,
    prec_hbm,
    hess_ref,
    pred_ref,
    columns_ref,
    counts_ref,
    diag_ref,
    logperm_ref,
    velocity_ref,
    direction_ref,
    obs_rows_ref,
    obs_weight_ref,
    prec_ref,
    blk,
    merged,
    diag_f,
    diag_a,
    obs_f,
    obs_a,
    part,
    zf,
    xf,
    rs_out,
    rs_in,
    yb,
    ad_out,
    ad_in,
    hb,
    pb,
    in_sem,
    blk_sem,
    xf_s,
    xf_r,
    rs_s,
    rs_r,
    yb_s,
    yb_r,
    ad_s,
    ad_r,
    hb_s,
    hb_r,
    pb_s,
    pb_r,
):
    row = lax.axis_index("row")
    col = lax.axis_index("col")
    quad = lax.div(row, jnp.int32(nmem))
    mem = lax.rem(row, jnp.int32(nmem))
    nrows, nslots, width = blk.shape[0], blk.shape[1], blk.shape[2]
    share = direction_ref.shape[0]
    nblk = nmem * nrows

    def device(q, k, c):
        return (q * nmem + k, c)

    def copy(src, dst, send, recv, target):
        return pltpu.make_async_remote_copy(
            src_ref=src,
            dst_ref=dst,
            send_sem=send,
            recv_sem=recv,
            device_id=target,
            device_id_type=pl.DeviceIdType.MESH,
        )

    def landed(slot, recv):
        copy(slot, slot, recv, recv, (row, col)).wait_recv()

    def block_row(piece, i):
        return piece[i * share : (i + 1) * share]

    def stack(pieces):
        return jnp.concatenate(pieces, axis=0)

    def diag_apply(pairs, piece):
        return stack([wide_matmul(block_row(piece, i), pairs[i]) for i in range(nrows)])

    barrier = pltpu.get_barrier_semaphore()
    peers = [((quad, mem, flip(col, e, ncol)), None) for e in range(1, ncol)]
    off = quad != col
    for f in range(ncol):
        for x in range(nmem):
            when = None if f or x else off
            peers.append(((flip(quad, f, ncol), flip(mem, x, nmem), quad), when))
            peers.append(((col, flip(mem, x, nmem), flip(col, f, ncol)), when))

    def greet(target):
        pl.semaphore_signal(
            barrier, inc=1, device_id=device(*target), device_id_type=pl.DeviceIdType.MESH
        )

    for target, when in peers:
        if when is None:
            greet(target)
        else:
            pl.when(when)(functools.partial(greet, target))
    greeted = sum(1 if when is None else when.astype(jnp.int32) for _, when in peers)
    sources = (
        (logperm_hbm, logperm_ref),
        (velocity_hbm, velocity_ref),
        (direction_hbm.at[pl.ds(col * share, share)], direction_ref),
        (diag_hbm, diag_ref),
        (columns_hbm, columns_ref),
        (counts_hbm, counts_ref),
        (obs_rows_hbm, obs_rows_ref),
        (obs_weight_hbm, obs_weight_ref),
        (prec_hbm, prec_ref),
    )
    inputs = [
        pltpu.make_async_copy(src, dst, in_sem.at[n]) for n, (src, dst) in enumerate(sources)
    ]
    for item in inputs:
        item.start()
    fetches = [
        pltpu.make_async_copy(blocks_hbm.at[i], blk.at[i], blk_sem.at[i]) for i in range(nrows)
    ]
    for fetch in fetches:
        fetch.start()

    for item in inputs[:4]:
        item.wait()
    alpha = jnp.exp(logperm_ref[...]) * velocity_ref[...]
    for i in range(nrows):
        high, low = split(diag_ref[i].T)
        diag_f[i, :, :width] = high
        diag_f[i, :, width:] = low
    mine = direction_ref[...]
    forcing = stack([-alpha[i : i + 1] * mine[:, i, :] for i in range(nrows)])
    base = diag_apply(diag_f, forcing)

    def merge(i):
        fetches[i].wait()
        count = counts_ref[0, i]
        target = [
            jnp.where(jnp.int32(k) < count, columns_ref[i, k], jnp.int32(-1))
            for k in range(nslots)
        ]

        def body(pair, carry):
            for half in range(2):
                j = pair * 2 + half
                total = jnp.zeros((width, width), F32)
                for k in range(nslots):
                    keep = jnp.where(target[k] == j, jnp.float32(1), jnp.float32(0))
                    total = total + keep * blk[i, k].astype(F32)
                at = pl.ds(pl.multiple_of(j * width, width), width)
                merged[i * width : (i + 1) * width, at] = total.astype(BF16)
            return carry

        lax.fori_loop(0, nblk // 2, body, 0)

    sent = []

    def start(item, when=None):
        if when is None:
            item.start()
        else:
            pl.when(when)(item.start)
        sent.append((item, when))

    def drain(items):
        for item, when in items:
            if when is None:
                item.wait_send()
            else:
                pl.when(when)(item.wait_send)

    def spread(t, piece):
        zf[t] = piece.astype(BF16)
        for f in reversed(range(ncol)):
            for x in range(nmem):
                start(
                    copy(
                        zf.at[t],
                        xf.at[t, mem, col],
                        xf_s.at[t, f, x],
                        xf_r.at[t, mem, col],
                        device(flip(quad, f, ncol), flip(mem, x, nmem), quad),
                    ),
                    None if f or x else off,
                )

        @pl.when(quad == col)
        def _():
            xf[t, mem, col] = zf[t]

    def column_state(t):
        for e in range(ncol):
            for x in range(nmem):
                k, c = flip(mem, x, nmem), flip(col, e, ncol)
                wait = functools.partial(landed, xf.at[t, k, c], xf_r.at[t, k, c])
                if e or x:
                    wait()
                else:
                    pl.when(off)(wait)
        lanes = []
        for k in range(nmem):
            pieces = [xf[t, k, c].astype(F32) for c in range(ncol)]
            for i in range(nrows):
                lanes.append(stack([block_row(piece, i) for piece in pieces]))
        return jnp.concatenate(lanes, axis=1).astype(BF16)

    def sum_over_columns(t, terms):
        for c in range(ncol):
            rows = terms[c * share : (c + 1) * share]
            piece = stack([rows[:, i * width : (i + 1) * width] for i in range(nrows)])
            part[t, c] = piece
            rs_out[t, c] = piece.astype(BF16)
        for e in range(1, ncol):
            c = flip(col, e, ncol)
            start(
                copy(
                    rs_out.at[t, c],
                    rs_in.at[t, col],
                    rs_s.at[t, e],
                    rs_r.at[t, col],
                    device(quad, mem, c),
                )
            )
        total = part[t, col]
        for e in range(1, ncol):
            c = flip(col, e, ncol)
            landed(rs_in.at[t, c], rs_r.at[t, c])
            total = total + rs_in[t, c].astype(F32)
        return total

    def gather_start(buf, at, send, recv):
        for e in range(1, ncol):
            start(
                copy(
                    buf.at[at + (col,)],
                    buf.at[at + (col,)],
                    send.at[at + (e,)],
                    recv.at[at + (col,)],
                    device(quad, mem, flip(col, e, ncol)),
                )
            )

    def gather_wait(buf, at, recv):
        for e in range(1, ncol):
            c = flip(col, e, ncol)
            landed(buf.at[at + (c,)], recv.at[at + (c,)])

    state = base
    for t in range(SWEEPS):
        if t == 0:
            pl.semaphore_wait(barrier, greeted)
        spread(t, state)
        if t == 0:
            for item in inputs[4:]:
                item.wait()
            for i in range(nrows):
                merge(i)
        terms = matmul_t(column_state(t), merged[...])
        if t == 0:
            for i in range(nrows):
                high, low = split(diag_ref[i])
                diag_a[i, :, :width] = high
                diag_a[i, :, width:] = low
            high, low = split(obs_weight_ref[...])
            points = obs_weight_ref.shape[0]
            obs_a[:, :width] = high
            obs_a[:, width:] = low
            high, low = split(obs_weight_ref[...].T)
            obs_f[:, :points] = high
            obs_f[:, points:] = low
        state = base - diag_apply(diag_f, sum_over_columns(t, terms))

    sampled = wide_matmul(state, obs_f[...])
    chosen = [(obs_rows_ref[...] == i).astype(F32) for i in range(nrows)]
    predicted = sum(block_row(sampled, i) * chosen[i] for i in range(nrows))
    weighted = predicted * prec_ref[...]
    force = -wide_matmul(stack([weighted * chosen[i] for i in range(nrows)]), obs_a[...])
    adjoint = diag_apply(diag_a, force)

    for t in range(SWEEPS):
        yb[t, col] = adjoint.astype(BF16)
        gather_start(yb, (t,), yb_s, yb_r)
        if t == 0:
            pb[col] = predicted
            gather_start(pb, (), pb_s, pb_r)
        gather_wait(yb, (t,), yb_r)
        pieces = [yb[t, c].astype(F32) for c in range(ncol)]
        lanes = [stack([block_row(piece, i) for piece in pieces]) for i in range(nrows)]
        terms = matmul(jnp.concatenate(lanes, axis=1).astype(BF16), merged[...])
        for k in range(nmem):
            for c in range(ncol):
                rows = terms[c * share : (c + 1) * share]
                ad_out[t, k, c] = stack(
                    [
                        rows[:, (k * nrows + i) * width : (k * nrows + i + 1) * width]
                        for i in range(nrows)
                    ]
                ).astype(BF16)
        for e in reversed(range(ncol)):
            for x in range(nmem):
                k, c = flip(mem, x, nmem), flip(col, e, ncol)
                start(
                    copy(
                        ad_out.at[t, k, c],
                        ad_in.at[t, mem, quad],
                        ad_s.at[t, x, e],
                        ad_r.at[t, mem, quad],
                        device(col, k, c),
                    ),
                    None if e or x else off,
                )

        @pl.when(quad == col)
        def _():
            ad_in[t, mem, quad] = ad_out[t, mem, col]

        total = 0.0
        for f in range(ncol):
            for x in range(nmem):
                k, q = flip(mem, x, nmem), flip(quad, f, ncol)
                wait = functools.partial(landed, ad_in.at[t, k, q], ad_r.at[t, k, q])
                if f or x:
                    wait()
                else:
                    pl.when(off)(wait)
                total = total + ad_in[t, k, q].astype(F32)
        adjoint = diag_apply(diag_a, force - total)

    hb[col] = stack(
        [-alpha[i : i + 1] * block_row(adjoint, i) for i in range(nrows)]
    ).astype(BF16)
    gather_start(hb, (), hb_s, hb_r)
    gather_wait(pb, (), pb_r)
    for c in range(ncol):
        pred_ref[c * share : (c + 1) * share, :] = pb[c]
    drain(sent[: 1 - ncol])
    gather_wait(hb, (), hb_r)
    for c in range(ncol):
        piece = hb[c].astype(F32)
        for i in range(nrows):
            hess_ref[c * share : (c + 1) * share, i, :] = block_row(piece, i)

    drain(sent[1 - ncol :])


def hand_over(hess_from, pred_from, hess_to, pred_to, sem):
    moves = [
        pltpu.make_async_copy(hess_from, hess_to, sem.at[0]),
        pltpu.make_async_copy(pred_from, pred_to, sem.at[1]),
    ]
    for move in moves:
        move.start()
    for move in moves:
        move.wait()


def per_device(
    blocks,
    columns,
    counts,
    inverse_diag,
    log_inverse_permeability,
    base_velocity,
    direction,
    obs_rows,
    obs_weight,
    noise_prec,
):
    ncol = lax.axis_size("col")
    nmem = lax.axis_size("row") // ncol
    nrows, nslots, width, _ = blocks.shape
    directions, points = direction.shape[0], obs_weight.shape[0]
    share = directions // ncol
    rows = nrows * share
    dma = pltpu.SemaphoreType.DMA
    vmem = pl.BlockSpec(memory_space=pltpu.VMEM)

    def pieces(*lead):
        return pltpu.VMEM(lead + (rows, width), BF16)

    s, c, g = SWEEPS, ncol, nmem
    results = pl.pallas_call(
        functools.partial(kernel, ncol, nmem),
        out_shape=(
            jax.ShapeDtypeStruct(direction.shape, F32),
            jax.ShapeDtypeStruct((directions, points), F32),
        ),
        in_specs=[pl.BlockSpec(memory_space=pl.ANY)] * 10,
        out_specs=(vmem, vmem),
        scratch_shapes=[
            pltpu.SMEM(columns.shape, jnp.int32),
            pltpu.SMEM((1, nrows), jnp.int32),
            pltpu.VMEM(inverse_diag.shape, F32),
            pltpu.VMEM(base_velocity.shape, F32),
            pltpu.VMEM(base_velocity.shape, F32),
            pltpu.VMEM((share,) + direction.shape[1:], F32),
            pltpu.VMEM((1, points), jnp.int32),
            pltpu.VMEM(obs_weight.shape, F32),
            pltpu.VMEM((1, points), F32),
            pltpu.VMEM(blocks.shape, BF16),
            pltpu.VMEM((nrows * width, nmem * nrows * width), BF16),
            pltpu.VMEM((nrows, width, 2 * width), BF16),
            pltpu.VMEM((nrows, width, 2 * width), BF16),
            pltpu.VMEM((width, 2 * points), BF16),
            pltpu.VMEM((points, 2 * width), BF16),
            pltpu.VMEM((s, c, rows, width), F32),
            pieces(s),
            pieces(s, g, c),
            pieces(s, c),
            pieces(s, c),
            pieces(s, c),
            pieces(s, g, c),
            pieces(s, g, c),
            pieces(c),
            pltpu.VMEM((c, share, points), F32),
            dma((9,)),
            dma((nrows,)),
            dma((s, c, g)),
            dma((s, g, c)),
            dma((s, c)),
            dma((s, c)),
            dma((s, c)),
            dma((s, c)),
            dma((s, g, c)),
            dma((s, g, c)),
            dma((c,)),
            dma((c,)),
            dma((c,)),
            dma((c,)),
        ],
        compiler_params=pltpu.CompilerParams(
            collective_id=0, has_side_effects=True, vmem_limit_bytes=60 * 1024 * 1024
        ),
    )(
        columns,
        counts.reshape(1, nrows),
        blocks,
        inverse_diag,
        log_inverse_permeability,
        base_velocity,
        direction,
        obs_rows.reshape(1, points),
        obs_weight,
        noise_prec.reshape(1, points),
    )
    anywhere = pl.BlockSpec(memory_space=pl.ANY)
    return pl.pallas_call(
        hand_over,
        out_shape=tuple(jax.ShapeDtypeStruct(x.shape, x.dtype) for x in results),
        in_specs=[anywhere] * 2,
        out_specs=(anywhere, anywhere),
        scratch_shapes=[dma((2,))],
        compiler_params=pltpu.CompilerParams(vmem_limit_bytes=60 * 1024 * 1024),
    )(*results)


def solution(mesh):
    placed = (
        P("row", "col", None, None),
        P("row", "col"),
        P("row", "col"),
        P("row", None, None),
        P("row", None),
        P("row", None),
        P(None, "row", None),
        P("row"),
        P("row", None),
        P("row"),
    )
    return jax.shard_map(
        per_device,
        mesh=mesh,
        in_specs=placed,
        out_specs=(P(None, "row", None), P(None, "row")),
        check_vma=False,
    )
```

```python
import functools

import jax
import jax.numpy as jnp
from jax import lax
from jax.experimental import pallas as pl
from jax.experimental.pallas import tpu as pltpu
from jax.sharding import PartitionSpec as P

F32 = jnp.float32
BF16 = jnp.bfloat16
SWEEPS = 2


def flip(index, bits, size):
    total, bit = 0, 1
    while bit < size:
        digit = lax.rem(lax.div(index, jnp.int32(bit)), jnp.int32(2))
        total = total + bit * (1 - digit if (bits // bit) % 2 else digit)
        bit *= 2
    return total


def split(values):
    high = values.astype(BF16)
    return high, (values - high.astype(F32)).astype(BF16)


def matmul(left, right):
    return lax.dot_general(left, right, (((1,), (0,)), ((), ())), preferred_element_type=F32)


def matmul_t(left, right):
    return lax.dot_general(left, right, (((1,), (1,)), ((), ())), preferred_element_type=F32)


def wide_matmul(values, pair):
    rows, width = values.shape[0], pair.shape[1] // 2
    high = values.astype(BF16).astype(F32)
    both = jnp.concatenate([high, values - high], axis=0).astype(BF16)
    out = matmul(both, pair)
    return out[:rows, :width] + out[:rows, width:] + out[rows:, :width]


def kernel(
    ncol,
    nmem,
    columns_hbm,
    counts_hbm,
    blocks_hbm,
    diag_hbm,
    logperm_hbm,
    velocity_hbm,
    direction_hbm,
    obs_rows_hbm,
    obs_weight_hbm,
    prec_hbm,
    hess_ref,
    pred_ref,
    columns_ref,
    counts_ref,
    diag_ref,
    logperm_ref,
    velocity_ref,
    direction_ref,
    obs_rows_ref,
    obs_weight_ref,
    prec_ref,
    blk,
    merged,
    diag_f,
    diag_a,
    obs_f,
    obs_a,
    part,
    zf,
    xf,
    rs_out,
    rs_in,
    yb,
    ad_out,
    ad_in,
    hb,
    whole,
    base_all,
    in_sem,
    blk_sem,
    xf_s,
    xf_r,
    rs_s,
    rs_r,
    yb_s,
    yb_r,
    ad_s,
    ad_r,
    hb_s,
    hb_r,
    whole_s,
    whole_r,
):
    row = lax.axis_index("row")
    col = lax.axis_index("col")
    quad = lax.div(row, jnp.int32(nmem))
    mem = lax.rem(row, jnp.int32(nmem))
    nrows, nslots, width = blk.shape[0], blk.shape[1], blk.shape[2]
    share = direction_ref.shape[0] // ncol
    nblk = nmem * nrows
    ndir = share * ncol

    def device(q, k, c):
        return (q * nmem + k, c)

    def copy(src, dst, send, recv, target):
        return pltpu.make_async_remote_copy(
            src_ref=src,
            dst_ref=dst,
            send_sem=send,
            recv_sem=recv,
            device_id=target,
            device_id_type=pl.DeviceIdType.MESH,
        )

    def landed(slot, recv):
        copy(slot, slot, recv, recv, (row, col)).wait_recv()

    def block_row(piece, i):
        return piece[i * share : (i + 1) * share]

    def stack(pieces):
        return jnp.concatenate(pieces, axis=0)

    def diag_apply(pairs, piece):
        return stack([wide_matmul(block_row(piece, i), pairs[i]) for i in range(nrows)])

    barrier = pltpu.get_barrier_semaphore()
    peers = [((quad, mem, flip(col, e, ncol)), None) for e in range(1, ncol)]
    off = quad != col
    for f in range(ncol):
        for x in range(nmem):
            when = None if f or x else off
            peers.append(((flip(quad, f, ncol), flip(mem, x, nmem), quad), when))
            peers.append(((col, flip(mem, x, nmem), flip(col, f, ncol)), when))

    def greet(target):
        pl.semaphore_signal(
            barrier, inc=1, device_id=device(*target), device_id_type=pl.DeviceIdType.MESH
        )

    for target, when in peers:
        if when is None:
            greet(target)
        else:
            pl.when(when)(functools.partial(greet, target))
    greeted = sum(1 if when is None else when.astype(jnp.int32) for _, when in peers)
    sources = (
        (logperm_hbm, logperm_ref),
        (velocity_hbm, velocity_ref),
        (direction_hbm, direction_ref),
        (diag_hbm, diag_ref),
        (columns_hbm, columns_ref),
        (counts_hbm, counts_ref),
        (obs_rows_hbm, obs_rows_ref),
        (obs_weight_hbm, obs_weight_ref),
        (prec_hbm, prec_ref),
    )
    inputs = [
        pltpu.make_async_copy(src, dst, in_sem.at[n]) for n, (src, dst) in enumerate(sources)
    ]
    for item in inputs:
        item.start()
    fetches = [
        pltpu.make_async_copy(blocks_hbm.at[i], blk.at[i], blk_sem.at[i]) for i in range(nrows)
    ]
    for fetch in fetches:
        fetch.start()

    for item in inputs[:4]:
        item.wait()
    alpha = jnp.exp(logperm_ref[...]) * velocity_ref[...]
    for i in range(nrows):
        high, low = split(diag_ref[i].T)
        diag_f[i, :, :width] = high
        diag_f[i, :, width:] = low
    mine = direction_ref[pl.ds(col * share, share)]
    forcing = stack([-alpha[i : i + 1] * mine[:, i, :] for i in range(nrows)])
    base = diag_apply(diag_f, forcing)

    def merge(i):
        fetches[i].wait()
        count = counts_ref[0, i]
        target = [
            jnp.where(jnp.int32(k) < count, columns_ref[i, k], jnp.int32(-1))
            for k in range(nslots)
        ]

        def body(pair, carry):
            for half in range(2):
                j = pair * 2 + half
                total = jnp.zeros((width, width), F32)
                for k in range(nslots):
                    keep = jnp.where(target[k] == j, jnp.float32(1), jnp.float32(0))
                    total = total + keep * blk[i, k].astype(F32)
                at = pl.ds(pl.multiple_of(j * width, width), width)
                merged[i * width : (i + 1) * width, at] = total.astype(BF16)
            return carry

        lax.fori_loop(0, nblk // 2, body, 0)
        high, low = split(diag_ref[i])
        own = slice(i * width, (i + 1) * width)
        both = matmul(jnp.concatenate([high, low], axis=0), merged[own, :])
        merged[own, :] = (both[:width] + both[width:]).astype(BF16)

    sent = []

    def start(item, when=None):
        if when is None:
            item.start()
        else:
            pl.when(when)(item.start)
        sent.append((item, when))

    def drain(items):
        for item, when in items:
            if when is None:
                item.wait_send()
            else:
                pl.when(when)(item.wait_send)

    def spread(t, piece):
        zf[t] = piece.astype(BF16)
        for f in reversed(range(ncol)):
            for x in range(nmem):
                start(
                    copy(
                        zf.at[t],
                        xf.at[t, mem, col],
                        xf_s.at[t, f, x],
                        xf_r.at[t, mem, col],
                        device(flip(quad, f, ncol), flip(mem, x, nmem), quad),
                    ),
                    None if f or x else off,
                )

        @pl.when(quad == col)
        def _():
            xf[t, mem, col] = zf[t]

    def column_state(t):
        for e in range(ncol):
            for x in range(nmem):
                k, c = flip(mem, x, nmem), flip(col, e, ncol)
                wait = functools.partial(landed, xf.at[t, k, c], xf_r.at[t, k, c])
                if e or x:
                    wait()
                else:
                    pl.when(off)(wait)
        lanes = []
        for k in range(nmem):
            pieces = [xf[t, k, c].astype(F32) for c in range(ncol)]
            for i in range(nrows):
                lanes.append(stack([block_row(piece, i) for piece in pieces]))
        return jnp.concatenate(lanes, axis=1).astype(BF16)

    def sum_start(t, terms):
        for c in range(ncol):
            rows = terms[c * share : (c + 1) * share]
            piece = stack([rows[:, i * width : (i + 1) * width] for i in range(nrows)])
            part[c] = piece
            rs_out[t, c] = piece.astype(BF16)
        for e in range(1, ncol):
            c = flip(col, e, ncol)
            start(
                copy(
                    rs_out.at[t, c],
                    rs_in.at[t, col],
                    rs_s.at[t, e],
                    rs_r.at[t, col],
                    device(quad, mem, c),
                )
            )

    def sum_finish(t):
        total = part[col]
        for e in range(1, ncol):
            c = flip(col, e, ncol)
            landed(rs_in.at[t, c], rs_r.at[t, c])
            total = total + rs_in[t, c].astype(F32)
        return total

    def by_block_row(values):
        return stack([values[:, i * width : (i + 1) * width] for i in range(nrows)])

    def by_lane(values):
        count = values.shape[0] // nrows
        return jnp.concatenate(
            [values[i * count : (i + 1) * count] for i in range(nrows)], axis=1
        )

    def gather_start(buf, at, send, recv):
        for e in range(1, ncol):
            start(
                copy(
                    buf.at[at + (col,)],
                    buf.at[at + (col,)],
                    send.at[at + (e,)],
                    recv.at[at + (col,)],
                    device(quad, mem, flip(col, e, ncol)),
                )
            )

    def gather_wait(buf, at, recv):
        for e in range(1, ncol):
            c = flip(col, e, ncol)
            landed(buf.at[at + (c,)], recv.at[at + (c,)])

    pl.semaphore_wait(barrier, greeted)
    spread(0, base)
    for item in inputs[4:]:
        item.wait()
    for i in range(nrows):
        merge(i)
    for t in range(SWEEPS - 1):
        sum_start(t, matmul_t(column_state(t), merged[...]))
        if t == 0:
            every = stack([-alpha[i : i + 1] * direction_ref[:, i, :] for i in range(nrows)])
            base_all[...] = by_lane(
                stack(
                    [
                        wide_matmul(every[i * ndir : (i + 1) * ndir], diag_f[i])
                        for i in range(nrows)
                    ]
                )
            )
            points = obs_weight_ref.shape[0]
            high, low = split(obs_weight_ref[...].T)
            obs_f[:, :points] = high
            obs_f[:, points:] = low
        spread(t + 1, base - sum_finish(t))

    terms = matmul_t(column_state(SWEEPS - 1), merged[...])
    whole[col] = terms.astype(BF16)
    for e in range(1, ncol):
        start(
            copy(
                whole.at[col],
                whole.at[col],
                whole_s.at[e],
                whole_r.at[col],
                device(quad, mem, flip(col, e, ncol)),
            )
        )
    high, low = split(obs_weight_ref[...])
    obs_a[:, :width] = high
    obs_a[:, width:] = low
    for e in range(1, ncol):
        c = flip(col, e, ncol)
        landed(whole.at[c], whole_r.at[c])
    state = base_all[...] - sum(whole[c].astype(F32) for c in range(ncol))

    sampled = wide_matmul(by_block_row(state), obs_f[...])
    chosen = [(obs_rows_ref[...] == i).astype(F32) for i in range(nrows)]
    predicted = sum(sampled[i * ndir : (i + 1) * ndir] * chosen[i] for i in range(nrows))
    weighted = predicted * prec_ref[...]
    force_all = by_lane(
        -wide_matmul(stack([weighted * chosen[i] for i in range(nrows)]), obs_a[...])
    )
    operand = force_all.astype(BF16)

    for t in range(SWEEPS):
        if t:
            yb[t, col] = adjoint.astype(BF16)
            gather_start(yb, (t,), yb_s, yb_r)
            gather_wait(yb, (t,), yb_r)
            pieces = [yb[t, c].astype(F32) for c in range(ncol)]
            operand = jnp.concatenate(
                [stack([block_row(piece, i) for piece in pieces]) for i in range(nrows)], axis=1
            ).astype(BF16)
        terms = matmul(operand, merged[...])
        for k in range(nmem):
            for c in range(ncol):
                rows = terms[c * share : (c + 1) * share]
                ad_out[t, k, c] = stack(
                    [
                        rows[:, (k * nrows + i) * width : (k * nrows + i + 1) * width]
                        for i in range(nrows)
                    ]
                ).astype(BF16)
        for e in reversed(range(ncol)):
            for x in range(nmem):
                k, c = flip(mem, x, nmem), flip(col, e, ncol)
                start(
                    copy(
                        ad_out.at[t, k, c],
                        ad_in.at[t, mem, quad],
                        ad_s.at[t, x, e],
                        ad_r.at[t, mem, quad],
                        device(col, k, c),
                    ),
                    None if e or x else off,
                )

        @pl.when(quad == col)
        def _():
            ad_in[t, mem, quad] = ad_out[t, mem, col]

        if t == 0:
            pred_ref[...] = predicted
            for c in range(ncol):
                part[c] = by_block_row(force_all[c * share : (c + 1) * share])
            force = part[col]
            for i in range(nrows):
                high, low = split(diag_ref[i])
                diag_a[i, :, :width] = high
                diag_a[i, :, width:] = low
        total = 0.0
        for f in range(ncol):
            for x in range(nmem):
                k, q = flip(mem, x, nmem), flip(quad, f, ncol)
                wait = functools.partial(landed, ad_in.at[t, k, q], ad_r.at[t, k, q])
                if f or x:
                    wait()
                else:
                    pl.when(off)(wait)
                total = total + ad_in[t, k, q].astype(F32)
        adjoint = force - total

    adjoint = diag_apply(diag_a, adjoint)
    hb[col] = stack(
        [-alpha[i : i + 1] * block_row(adjoint, i) for i in range(nrows)]
    ).astype(BF16)
    gather_start(hb, (), hb_s, hb_r)
    drain(sent[: 1 - ncol])
    gather_wait(hb, (), hb_r)
    for c in range(ncol):
        piece = hb[c].astype(F32)
        for i in range(nrows):
            hess_ref[c * share : (c + 1) * share, i, :] = block_row(piece, i)

    drain(sent[1 - ncol :])


def per_device(
    blocks,
    columns,
    counts,
    inverse_diag,
    log_inverse_permeability,
    base_velocity,
    direction,
    obs_rows,
    obs_weight,
    noise_prec,
):
    ncol = lax.axis_size("col")
    nmem = lax.axis_size("row") // ncol
    nrows, nslots, width, _ = blocks.shape
    directions, points = direction.shape[0], obs_weight.shape[0]
    share = directions // ncol
    rows = nrows * share
    dma = pltpu.SemaphoreType.DMA
    vmem = pl.BlockSpec(memory_space=pltpu.VMEM)

    def pieces(*lead):
        return pltpu.VMEM(lead + (rows, width), BF16)

    s, c, g = SWEEPS, ncol, nmem
    return pl.pallas_call(
        functools.partial(kernel, ncol, nmem),
        out_shape=(
            jax.ShapeDtypeStruct(direction.shape, F32),
            jax.ShapeDtypeStruct((directions, points), F32),
        ),
        in_specs=[pl.BlockSpec(memory_space=pl.ANY)] * 10,
        out_specs=(vmem, vmem),
        scratch_shapes=[
            pltpu.SMEM(columns.shape, jnp.int32),
            pltpu.SMEM((1, nrows), jnp.int32),
            pltpu.VMEM(inverse_diag.shape, F32),
            pltpu.VMEM(base_velocity.shape, F32),
            pltpu.VMEM(base_velocity.shape, F32),
            pltpu.VMEM(direction.shape, F32),
            pltpu.VMEM((1, points), jnp.int32),
            pltpu.VMEM(obs_weight.shape, F32),
            pltpu.VMEM((1, points), F32),
            pltpu.VMEM(blocks.shape, BF16),
            pltpu.VMEM((nrows * width, nmem * nrows * width), BF16),
            pltpu.VMEM((nrows, width, 2 * width), BF16),
            pltpu.VMEM((nrows, width, 2 * width), BF16),
            pltpu.VMEM((width, 2 * points), BF16),
            pltpu.VMEM((points, 2 * width), BF16),
            pltpu.VMEM((c, rows, width), F32),
            pieces(s),
            pieces(s, g, c),
            pieces(s, c),
            pieces(s, c),
            pieces(s, c),
            pieces(s, g, c),
            pieces(s, g, c),
            pieces(c),
            pltpu.VMEM((c, directions, nrows * width), BF16),
            pltpu.VMEM((directions, nrows * width), F32),
            dma((9,)),
            dma((nrows,)),
            dma((s, c, g)),
            dma((s, g, c)),
            dma((s, c)),
            dma((s, c)),
            dma((s, c)),
            dma((s, c)),
            dma((s, g, c)),
            dma((s, g, c)),
            dma((c,)),
            dma((c,)),
            dma((c,)),
            dma((c,)),
        ],
        compiler_params=pltpu.CompilerParams(
            collective_id=0, has_side_effects=True, vmem_limit_bytes=60 * 1024 * 1024
        ),
    )(
        columns,
        counts.reshape(1, nrows),
        blocks,
        inverse_diag,
        log_inverse_permeability,
        base_velocity,
        direction,
        obs_rows.reshape(1, points),
        obs_weight,
        noise_prec.reshape(1, points),
    )


def solution(mesh):
    placed = (
        P("row", "col", None, None),
        P("row", "col"),
        P("row", "col"),
        P("row", None, None),
        P("row", None),
        P("row", None),
        P(None, "row", None),
        P("row"),
        P("row", None),
        P("row"),
    )
    return jax.shard_map(
        per_device,
        mesh=mesh,
        in_specs=placed,
        out_specs=(P(None, "row", None), P(None, "row")),
        check_vma=False,
    )
```

```python
import functools

import jax
import jax.numpy as jnp
from jax import lax
from jax.experimental import pallas as pl
from jax.experimental.pallas import tpu as pltpu
from jax.sharding import PartitionSpec as P

F32 = jnp.float32
BF16 = jnp.bfloat16
SWEEPS = 2


def flip(index, bits, size):
    total, bit = 0, 1
    while bit < size:
        digit = lax.rem(lax.div(index, jnp.int32(bit)), jnp.int32(2))
        total = total + bit * (1 - digit if (bits // bit) % 2 else digit)
        bit *= 2
    return total


def split(values):
    high = values.astype(BF16)
    return high, (values - high.astype(F32)).astype(BF16)


def matmul(left, right):
    return lax.dot_general(left, right, (((1,), (0,)), ((), ())), preferred_element_type=F32)


def matmul_t(left, right):
    return lax.dot_general(left, right, (((1,), (1,)), ((), ())), preferred_element_type=F32)


def wide_matmul(values, pair):
    rows, width = values.shape[0], pair.shape[1] // 2
    high = values.astype(BF16).astype(F32)
    both = jnp.concatenate([high, values - high], axis=0).astype(BF16)
    out = matmul(both, pair)
    return out[:rows, :width] + out[:rows, width:] + out[rows:, :width]


def kernel(
    ncol,
    nmem,
    columns_hbm,
    counts_hbm,
    blocks_hbm,
    diag_hbm,
    logperm_hbm,
    velocity_hbm,
    direction_hbm,
    obs_rows_hbm,
    obs_weight_hbm,
    prec_hbm,
    hess_ref,
    pred_ref,
    columns_ref,
    counts_ref,
    diag_ref,
    logperm_ref,
    velocity_ref,
    direction_ref,
    obs_rows_ref,
    obs_weight_ref,
    prec_ref,
    blk,
    merged,
    diag_f,
    diag_a,
    obs_f,
    obs_a,
    part,
    zf,
    xf,
    rs_out,
    rs_in,
    yb,
    ad_out,
    ad_in,
    hb,
    whole,
    base_all,
    in_sem,
    blk_sem,
    xf_s,
    xf_r,
    rs_s,
    rs_r,
    yb_s,
    yb_r,
    ad_s,
    ad_r,
    hb_s,
    hb_r,
    whole_s,
    whole_r,
):
    row = lax.axis_index("row")
    col = lax.axis_index("col")
    quad = lax.div(row, jnp.int32(nmem))
    mem = lax.rem(row, jnp.int32(nmem))
    nrows, nslots, width = blk.shape[0], blk.shape[1], blk.shape[2]
    share = direction_ref.shape[0] // ncol
    nblk = nmem * nrows
    chunk = 32
    ndir = share * ncol

    def device(q, k, c):
        return (q * nmem + k, c)

    def copy(src, dst, send, recv, target):
        return pltpu.make_async_remote_copy(
            src_ref=src,
            dst_ref=dst,
            send_sem=send,
            recv_sem=recv,
            device_id=target,
            device_id_type=pl.DeviceIdType.MESH,
        )

    def landed(slot, recv):
        copy(slot, slot, recv, recv, (row, col)).wait_recv()

    def block_row(piece, i):
        return piece[i * share : (i + 1) * share]

    def stack(pieces):
        return jnp.concatenate(pieces, axis=0)

    def diag_apply(pairs, piece):
        return stack([wide_matmul(block_row(piece, i), pairs[i]) for i in range(nrows)])

    barrier = pltpu.get_barrier_semaphore()
    peers = [((quad, mem, flip(col, e, ncol)), None) for e in range(1, ncol)]
    off = quad != col
    for f in range(ncol):
        for x in range(nmem):
            when = None if f or x else off
            peers.append(((flip(quad, f, ncol), flip(mem, x, nmem), quad), when))
            peers.append(((col, flip(mem, x, nmem), flip(col, f, ncol)), when))

    def greet(target):
        pl.semaphore_signal(
            barrier, inc=1, device_id=device(*target), device_id_type=pl.DeviceIdType.MESH
        )

    for target, when in peers:
        if when is None:
            greet(target)
        else:
            pl.when(when)(functools.partial(greet, target))
    greeted = sum(1 if when is None else when.astype(jnp.int32) for _, when in peers)
    sources = (
        (logperm_hbm, logperm_ref),
        (velocity_hbm, velocity_ref),
        (direction_hbm, direction_ref),
        (diag_hbm, diag_ref),
        (columns_hbm, columns_ref),
        (counts_hbm, counts_ref),
        (obs_rows_hbm, obs_rows_ref),
        (obs_weight_hbm, obs_weight_ref),
        (prec_hbm, prec_ref),
    )
    inputs = [
        pltpu.make_async_copy(src, dst, in_sem.at[n]) for n, (src, dst) in enumerate(sources)
    ]
    for item in inputs:
        item.start()
    fetches = [
        pltpu.make_async_copy(blocks_hbm.at[i], blk.at[i], blk_sem.at[i]) for i in range(nrows)
    ]
    for fetch in fetches:
        fetch.start()

    for item in inputs[:4]:
        item.wait()
    alpha = jnp.exp(logperm_ref[...]) * velocity_ref[...]
    for i in range(nrows):
        high, low = split(diag_ref[i].T)
        diag_f[i, :, :width] = high
        diag_f[i, :, width:] = low
    mine = direction_ref[pl.ds(col * share, share)]
    forcing = stack([-alpha[i : i + 1] * mine[:, i, :] for i in range(nrows)])
    base = diag_apply(diag_f, forcing)

    def merge(i):
        fetches[i].wait()
        count = counts_ref[0, i]
        target = [
            jnp.where(jnp.int32(k) < count, columns_ref[i, k], jnp.int32(-1))
            for k in range(nslots)
        ]

        def body(step, carry):
            rows = pl.ds(pl.multiple_of(step * chunk, chunk), chunk)
            totals = [jnp.zeros((chunk, width), F32) for _ in range(nblk)]
            for k in range(nslots):
                values = blk[i, k, rows, :].astype(F32)
                for j in range(nblk):
                    keep = jnp.where(target[k] == j, jnp.float32(1), jnp.float32(0))
                    totals[j] = totals[j] + keep * values
            at = pl.ds(pl.multiple_of(i * width + step * chunk, chunk), chunk)
            for j in range(nblk):
                merged[at, j * width : (j + 1) * width] = totals[j].astype(BF16)
            return carry

        lax.fori_loop(0, width // chunk, body, 0)
        high, low = split(diag_ref[i])
        own = slice(i * width, (i + 1) * width)
        both = matmul(jnp.concatenate([high, low], axis=0), merged[own, :])
        merged[own, :] = (both[:width] + both[width:]).astype(BF16)

    sent = []

    def start(item, when=None):
        if when is None:
            item.start()
        else:
            pl.when(when)(item.start)
        sent.append((item, when))

    def drain(items):
        for item, when in items:
            if when is None:
                item.wait_send()
            else:
                pl.when(when)(item.wait_send)

    def spread(t, piece):
        zf[t] = piece.astype(BF16)
        for f in reversed(range(ncol)):
            for x in range(nmem):
                start(
                    copy(
                        zf.at[t],
                        xf.at[t, mem, col],
                        xf_s.at[t, f, x],
                        xf_r.at[t, mem, col],
                        device(flip(quad, f, ncol), flip(mem, x, nmem), quad),
                    ),
                    None if f or x else off,
                )

        @pl.when(quad == col)
        def _():
            xf[t, mem, col] = zf[t]

    def column_state(t):
        for e in range(ncol):
            for x in range(nmem):
                k, c = flip(mem, x, nmem), flip(col, e, ncol)
                wait = functools.partial(landed, xf.at[t, k, c], xf_r.at[t, k, c])
                if e or x:
                    wait()
                else:
                    pl.when(off)(wait)
        lanes = []
        for k in range(nmem):
            pieces = [xf[t, k, c].astype(F32) for c in range(ncol)]
            for i in range(nrows):
                lanes.append(stack([block_row(piece, i) for piece in pieces]))
        return jnp.concatenate(lanes, axis=1).astype(BF16)

    def sum_start(t, terms):
        for c in range(ncol):
            rows = terms[c * share : (c + 1) * share]
            piece = stack([rows[:, i * width : (i + 1) * width] for i in range(nrows)])
            part[c] = piece
            rs_out[t, c] = piece.astype(BF16)
        for e in range(1, ncol):
            c = flip(col, e, ncol)
            start(
                copy(
                    rs_out.at[t, c],
                    rs_in.at[t, col],
                    rs_s.at[t, e],
                    rs_r.at[t, col],
                    device(quad, mem, c),
                )
            )

    def sum_finish(t):
        total = part[col]
        for e in range(1, ncol):
            c = flip(col, e, ncol)
            landed(rs_in.at[t, c], rs_r.at[t, c])
            total = total + rs_in[t, c].astype(F32)
        return total

    def by_block_row(values):
        return stack([values[:, i * width : (i + 1) * width] for i in range(nrows)])

    def by_lane(values):
        count = values.shape[0] // nrows
        return jnp.concatenate(
            [values[i * count : (i + 1) * count] for i in range(nrows)], axis=1
        )

    def gather_start(buf, at, send, recv):
        for e in range(1, ncol):
            start(
                copy(
                    buf.at[at + (col,)],
                    buf.at[at + (col,)],
                    send.at[at + (e,)],
                    recv.at[at + (col,)],
                    device(quad, mem, flip(col, e, ncol)),
                )
            )

    def gather_wait(buf, at, recv):
        for e in range(1, ncol):
            c = flip(col, e, ncol)
            landed(buf.at[at + (c,)], recv.at[at + (c,)])

    pl.semaphore_wait(barrier, greeted)
    spread(0, base)
    for item in inputs[4:]:
        item.wait()
    for i in range(nrows):
        merge(i)
    for t in range(SWEEPS - 1):
        sum_start(t, matmul_t(column_state(t), merged[...]))
        if t == 0:
            every = stack([-alpha[i : i + 1] * direction_ref[:, i, :] for i in range(nrows)])
            base_all[...] = by_lane(
                stack(
                    [
                        wide_matmul(every[i * ndir : (i + 1) * ndir], diag_f[i])
                        for i in range(nrows)
                    ]
                )
            )
            points = obs_weight_ref.shape[0]
            high, low = split(obs_weight_ref[...].T)
            obs_f[:, :points] = high
            obs_f[:, points:] = low
        spread(t + 1, base - sum_finish(t))

    terms = matmul_t(column_state(SWEEPS - 1), merged[...])
    whole[col] = terms.astype(BF16)
    for e in range(1, ncol):
        start(
            copy(
                whole.at[col],
                whole.at[col],
                whole_s.at[e],
                whole_r.at[col],
                device(quad, mem, flip(col, e, ncol)),
            )
        )
    high, low = split(obs_weight_ref[...])
    obs_a[:, :width] = high
    obs_a[:, width:] = low
    for e in range(1, ncol):
        c = flip(col, e, ncol)
        landed(whole.at[c], whole_r.at[c])
    state = base_all[...] - sum(whole[c].astype(F32) for c in range(ncol))

    sampled = wide_matmul(by_block_row(state), obs_f[...])
    chosen = [(obs_rows_ref[...] == i).astype(F32) for i in range(nrows)]
    predicted = sum(sampled[i * ndir : (i + 1) * ndir] * chosen[i] for i in range(nrows))
    weighted = predicted * prec_ref[...]
    force_all = by_lane(
        -wide_matmul(stack([weighted * chosen[i] for i in range(nrows)]), obs_a[...])
    )
    operand = force_all.astype(BF16)

    for t in range(SWEEPS):
        if t:
            yb[t, col] = adjoint.astype(BF16)
            gather_start(yb, (t,), yb_s, yb_r)
            gather_wait(yb, (t,), yb_r)
            pieces = [yb[t, c].astype(F32) for c in range(ncol)]
            operand = jnp.concatenate(
                [stack([block_row(piece, i) for piece in pieces]) for i in range(nrows)], axis=1
            ).astype(BF16)
        terms = matmul(operand, merged[...])
        for k in range(nmem):
            for c in range(ncol):
                rows = terms[c * share : (c + 1) * share]
                ad_out[t, k, c] = stack(
                    [
                        rows[:, (k * nrows + i) * width : (k * nrows + i + 1) * width]
                        for i in range(nrows)
                    ]
                ).astype(BF16)
        for e in reversed(range(ncol)):
            for x in range(nmem):
                k, c = flip(mem, x, nmem), flip(col, e, ncol)
                start(
                    copy(
                        ad_out.at[t, k, c],
                        ad_in.at[t, mem, quad],
                        ad_s.at[t, x, e],
                        ad_r.at[t, mem, quad],
                        device(col, k, c),
                    ),
                    None if e or x else off,
                )

        @pl.when(quad == col)
        def _():
            ad_in[t, mem, quad] = ad_out[t, mem, col]

        if t == 0:
            pred_ref[...] = predicted
            for c in range(ncol):
                part[c] = by_block_row(force_all[c * share : (c + 1) * share])
            force = part[col]
            for i in range(nrows):
                high, low = split(diag_ref[i])
                diag_a[i, :, :width] = high
                diag_a[i, :, width:] = low
        total = 0.0
        for f in range(ncol):
            for x in range(nmem):
                k, q = flip(mem, x, nmem), flip(quad, f, ncol)
                wait = functools.partial(landed, ad_in.at[t, k, q], ad_r.at[t, k, q])
                if f or x:
                    wait()
                else:
                    pl.when(off)(wait)
                total = total + ad_in[t, k, q].astype(F32)
        adjoint = force - total

    adjoint = diag_apply(diag_a, adjoint)
    hb[col] = stack(
        [-alpha[i : i + 1] * block_row(adjoint, i) for i in range(nrows)]
    ).astype(BF16)
    gather_start(hb, (), hb_s, hb_r)
    drain(sent[: 1 - ncol])
    gather_wait(hb, (), hb_r)
    for c in range(ncol):
        piece = hb[c].astype(F32)
        for i in range(nrows):
            hess_ref[c * share : (c + 1) * share, i, :] = block_row(piece, i)

    drain(sent[1 - ncol :])


def per_device(
    blocks,
    columns,
    counts,
    inverse_diag,
    log_inverse_permeability,
    base_velocity,
    direction,
    obs_rows,
    obs_weight,
    noise_prec,
):
    ncol = lax.axis_size("col")
    nmem = lax.axis_size("row") // ncol
    nrows, nslots, width, _ = blocks.shape
    directions, points = direction.shape[0], obs_weight.shape[0]
    share = directions // ncol
    rows = nrows * share
    dma = pltpu.SemaphoreType.DMA
    vmem = pl.BlockSpec(memory_space=pltpu.VMEM)

    def pieces(*lead):
        return pltpu.VMEM(lead + (rows, width), BF16)

    s, c, g = SWEEPS, ncol, nmem
    return pl.pallas_call(
        functools.partial(kernel, ncol, nmem),
        out_shape=(
            jax.ShapeDtypeStruct(direction.shape, F32),
            jax.ShapeDtypeStruct((directions, points), F32),
        ),
        in_specs=[pl.BlockSpec(memory_space=pl.ANY)] * 10,
        out_specs=(vmem, vmem),
        scratch_shapes=[
            pltpu.SMEM(columns.shape, jnp.int32),
            pltpu.SMEM((1, nrows), jnp.int32),
            pltpu.VMEM(inverse_diag.shape, F32),
            pltpu.VMEM(base_velocity.shape, F32),
            pltpu.VMEM(base_velocity.shape, F32),
            pltpu.VMEM(direction.shape, F32),
            pltpu.VMEM((1, points), jnp.int32),
            pltpu.VMEM(obs_weight.shape, F32),
            pltpu.VMEM((1, points), F32),
            pltpu.VMEM(blocks.shape, BF16),
            pltpu.VMEM((nrows * width, nmem * nrows * width), BF16),
            pltpu.VMEM((nrows, width, 2 * width), BF16),
            pltpu.VMEM((nrows, width, 2 * width), BF16),
            pltpu.VMEM((width, 2 * points), BF16),
            pltpu.VMEM((points, 2 * width), BF16),
            pltpu.VMEM((c, rows, width), F32),
            pieces(s),
            pieces(s, g, c),
            pieces(s, c),
            pieces(s, c),
            pieces(s, c),
            pieces(s, g, c),
            pieces(s, g, c),
            pieces(c),
            pltpu.VMEM((c, directions, nrows * width), BF16),
            pltpu.VMEM((directions, nrows * width), F32),
            dma((9,)),
            dma((nrows,)),
            dma((s, c, g)),
            dma((s, g, c)),
            dma((s, c)),
            dma((s, c)),
            dma((s, c)),
            dma((s, c)),
            dma((s, g, c)),
            dma((s, g, c)),
            dma((c,)),
            dma((c,)),
            dma((c,)),
            dma((c,)),
        ],
        compiler_params=pltpu.CompilerParams(
            collective_id=0, has_side_effects=True, vmem_limit_bytes=60 * 1024 * 1024
        ),
    )(
        columns,
        counts.reshape(1, nrows),
        blocks,
        inverse_diag,
        log_inverse_permeability,
        base_velocity,
        direction,
        obs_rows.reshape(1, points),
        obs_weight,
        noise_prec.reshape(1, points),
    )


def solution(mesh):
    placed = (
        P("row", "col", None, None),
        P("row", "col"),
        P("row", "col"),
        P("row", None, None),
        P("row", None),
        P("row", None),
        P(None, "row", None),
        P("row"),
        P("row", None),
        P("row"),
    )
    return jax.shard_map(
        per_device,
        mesh=mesh,
        in_specs=placed,
        out_specs=(P(None, "row", None), P(None, "row")),
        check_vma=False,
    )
```
